32 devices in a mesh: dp: 4 (over y, x), mp: 8 (over z, core).
Axes of the slice: x: 2, y: 2, z: 4, core: 2. Of those that a mesh axis runs over, the one named last changes fastest.
Arguments:
- hidden_in: bfloat16 [8192, 2048], P(('dp', 'mp')), may hold values from -6 to 6
- cotangent: bfloat16 [8192, 2048], P(('dp', 'mp')), may hold values from -6 to 6
- domain_tags: int32 [4], P('dp'), may hold values from 0 to 2
- mix_weight: bfloat16 [2, 2048, 3, 2048], P(None, None, None, 'mp'), may hold values from -0.125 to 0.125
- mix_out_weight: bfloat16 [2, 2048, 2048], P(None, 'mp'), may hold values from -0.125 to 0.125
- glu_weight: bfloat16 [2, 2048, 2, 5632], P(None, None, None, 'mp'), may hold values from -0.125 to 0.125
- glu_out_weight: bfloat16 [2, 5632, 2048], P(None, 'mp'), may hold values from -0.078125 to 0.078125
- mix_gain: float32 [2, 2048], replicated, may hold values from 0.5 to 1.5
- out_gain: float32 [2, 2048], P(None, 'mp'), may hold values from 0.5 to 1.5
- glu_gain: float32 [2, 2048], replicated, may hold values from 0.5 to 1.5
- bound_logits: float32 [3, 2048], P(None, 'mp'), may hold values from -4 to 4
Outputs:
- hidden_out: float32 [8192, 2048], P(('dp', 'mp'))
- input_grad: float32 [8192, 2048], P(('dp', 'mp'))
- mix_weight_grad: float32 [2, 2048, 3, 2048], P(None, None, None, 'mp')
- mix_out_grad: float32 [2, 2048, 2048], P(None, 'mp')
- glu_weight_grad: float32 [2, 2048, 2, 5632], P(None, None, None, 'mp')
- glu_out_grad: float32 [2, 5632, 2048], P(None, 'mp')
- mix_gain_grad: float32 [2, 2048], replicated
- out_gain_grad: float32 [2, 2048], P(None, 'mp')
- glu_gain_grad: float32 [2, 2048], replicated
- bound_grad: float32 [3, 2048], P(None, 'mp')
The draws below stay inside these ranges and needn't reach their ends.
All inputs are finite; a program needn't handle non-finite values.
Results may differ from the reference program's by a relative error of at most 0.034.
Values may be sent and summed in bfloat16 or wider, within the bound.
No kernel may reach another device: no remote copies, remote signals or barrier semaphores. Data moves between devices by JAX's collectives and lax.ppermute only.
A program may use at most 384 MiB of HBM per device.

```python
import jax
import jax.numpy as jnp
from jax import lax

D = 2048
FF = 5632
LAYERS = 2
LEN = 2048
SEQ_GROUP = 1
BOUNDS = 3
SEQS = 4
TOKENS = 8192
N_DP = 4


def touch_ends(values, stream_key, smallest, top_value):
    place = [jax.random.randint(jax.random.fold_in(stream_key, axis), (), 0, length) for axis, length in enumerate(values.shape)]
    longest = values.shape.index(max(values.shape))
    next_to = place[:longest] + [(place[longest] + 1) % values.shape[longest]] + place[longest + 1:]
    return values.at[tuple(place)].set(smallest).at[tuple(next_to)].set(top_value)


def steps_of(own_key, shape, split, low, high):
    level = 1.0
    for position, parts in split:
        steps = jax.random.uniform(jax.random.fold_in(jax.random.fold_in(own_key, 6), position), (parts,), jnp.float32, low / len(split), high / len(split))
        level = level * jnp.repeat(jnp.exp(steps), shape[position] // parts).reshape((-1,) + (1,) * (len(shape) - 1 - position))
    return level


def gaussian(key, dims, spread, reach, pieces=(), held_as=jnp.bfloat16):
    loudness = steps_of(key, dims, pieces, -0.22, 0.18) if pieces else 1.0
    values = jax.random.normal(key, dims, jnp.float32) * spread * loudness
    return jnp.minimum(jnp.maximum(values, -reach), reach).astype(held_as)


def setup_inputs(seed: int = 0) -> dict:
    key_list = jax.random.split(jax.random.key(seed), 12)
    return {
        "hidden_in": gaussian(key_list[0], (TOKENS, D), 1.0, 6.0, ((0, 32),)),
        "cotangent": gaussian(key_list[1], (TOKENS, D), 1.0, 6.0, ((0, 32),)),
        "domain_tags": touch_ends(jax.random.randint(key_list[2], (SEQS,), 0, 3), jax.random.fold_in(key_list[2], 1), 0, 2).astype(jnp.int32),
        "mix_weight": gaussian(key_list[3], (LAYERS, D, 3, D), D ** -0.5, 0.125, ((3, 8),)),
        "mix_out_weight": gaussian(key_list[4], (LAYERS, D, D), D ** -0.5, 0.125, ((1, 8),)),
        "glu_weight": gaussian(key_list[5], (LAYERS, D, 2, FF), D ** -0.5, 0.125, ((3, 8),)),
        "glu_out_weight": gaussian(key_list[6], (LAYERS, FF, D), FF ** -0.5, 0.078125, ((1, 8),)),
        "mix_gain": jnp.clip(1.0 + 0.1 * jax.random.normal(key_list[7], (LAYERS, D), jnp.float32), 0.5, 1.5),
        "out_gain": jnp.clip(1.0 + 0.1 * jax.random.normal(key_list[8], (LAYERS, D), jnp.float32), 0.5, 1.5),
        "glu_gain": jnp.clip(1.0 + 0.1 * jax.random.normal(key_list[9], (LAYERS, D), jnp.float32), 0.5, 1.5),
        "bound_logits": gaussian(key_list[10], (BOUNDS, D), 1.0, 4.0, ((1, 8),), jnp.float32),
    }


@jax.custom_vjp
def low(v):
    return lax.optimization_barrier(v.astype(jnp.bfloat16)).astype(jnp.float32)

@jax.custom_vjp
def low_back(v):
    return v

def low_keep(v):
    return (low(v), None)

def low_pass(kept, grad):
    return (grad,)

def back_keep(v):
    return (v, None)

def back_low(kept, grad):
    return (low(grad),)
low.defvjp(low_keep, low_pass)
low_back.defvjp(back_keep, back_low)
norm_eps = 1e-06
domain_scale = (1.0, 0.5, 2.0)

def scaled_rms(values, gain_vec):
    return values * lax.rsqrt(lax.optimization_barrier(jnp.mean(values * values, -1, keepdims=True)) + norm_eps) * gain_vec

def bound_rows(logits):
    return jnp.cumsum(jax.nn.softmax(logits, 0), 0)

def recurrence(projected, lower_bound, seq_count):
    inputs = projected[:, 0]
    forget_pre = projected[:, 1]
    gate_pre = projected[:, 2]
    forget = lower_bound + (1.0 - lower_bound) * jax.nn.sigmoid(forget_pre)
    update = (1.0 - forget) * jax.nn.silu(inputs)
    seq_shape = (seq_count, -1, projected.shape[2])

    def combine(earlier, later_part):
        return (earlier[0] * later_part[0], later_part[0] * earlier[1] + later_part[1])
    scanned = lax.associative_scan(combine, (forget.reshape(seq_shape), update.reshape(seq_shape)), axis=1)
    return scanned[1].reshape(update.shape) * jax.nn.silu(gate_pre)

def glu_act(gate_up):
    return jax.nn.silu(gate_up[:, 0]) * gate_up[:, 1]

def highest(left, right):
    return jnp.dot(left, right, precision=lax.Precision.HIGHEST)

def residual_block(stream, weights_layer, lower_bound, seq_count):
    w_mix, w_out, w_glu, w_down, gain_mix, gain_out, gain_glu = weights_layer
    row_count = stream.shape[0]
    width = stream.shape[1]
    mixer_in = low(scaled_rms(stream, gain_mix))
    projected = low_back(highest(mixer_in, w_mix.reshape(width, -1))).reshape(row_count, 3, width)
    mixed = low(scaled_rms(recurrence(projected, lower_bound, seq_count), gain_out))
    stream_mid = stream + low_back(highest(mixed, w_out))
    glu_in = low(scaled_rms(stream_mid, gain_glu))
    gate_up = low_back(highest(glu_in, w_glu.reshape(width, -1))).reshape(row_count, 2, -1)
    hidden = low(glu_act(gate_up))
    return stream_mid + low_back(highest(hidden, w_down))

def forward(stream, weights_all, seq_count):
    mix_weight, mix_out_weight, glu_weight, glu_out_weight, mix_gain, out_gain, glu_gain, bound_logits = weights_all
    bounds = bound_rows(bound_logits)
    for layer_index in range(mix_weight.shape[0]):
        weights_layer = (mix_weight[layer_index], mix_out_weight[layer_index], glu_weight[layer_index], glu_out_weight[layer_index], mix_gain[layer_index], out_gain[layer_index], glu_gain[layer_index])
        stream = residual_block(stream, weights_layer, bounds[layer_index], seq_count)
    return stream

def reference(hidden_in, cotangent, domain_tags, mix_weight, mix_out_weight, glu_weight, glu_out_weight, mix_gain, out_gain, glu_gain, bound_logits):
    weights_all = tuple((item.astype(jnp.float32) for item in (mix_weight, mix_out_weight, glu_weight, glu_out_weight, mix_gain, out_gain, glu_gain, bound_logits)))
    width = hidden_in.shape[1]
    inputs_grouped = hidden_in.astype(jnp.float32).reshape(N_DP, -1, width)
    cot_grouped = cotangent.astype(jnp.float32).reshape(N_DP, -1, width)
    tags_grouped = domain_tags.reshape(N_DP, SEQ_GROUP)
    scale_table = jnp.array(domain_scale, dtype=jnp.float32)

    def group_step(grad_total, group_data):
        group_in, group_cot, group_tags = group_data
        matches = group_tags[:, None] == jnp.arange(3, dtype=jnp.int32)[None, :]
        seq_scale = lax.optimization_barrier(jnp.sum(jnp.where(matches, scale_table[None, :], 0.0), -1))
        row_scale = jnp.repeat(seq_scale, LEN)
        outputs, pullback = jax.vjp(lambda stream_in, weights_in: forward(stream_in, weights_in, SEQ_GROUP), group_in, weights_all)
        input_grad, weight_grads = pullback(group_cot * row_scale[:, None])
        grad_total = jax.tree.map(lambda acc_val, new_val: acc_val + new_val, grad_total, weight_grads)
        return (grad_total, (outputs, input_grad))
    zero_grads = jax.tree.map(jnp.zeros_like, weights_all)
    grad_total, stacked = lax.scan(group_step, zero_grads, (inputs_grouped, cot_grouped, tags_grouped))
    return (stacked[0].reshape(-1, width), stacked[1].reshape(-1, width), grad_total[0], grad_total[1], grad_total[2], grad_total[3], grad_total[4], grad_total[5], grad_total[6], grad_total[7])
```

```python
import functools

import jax
import jax.numpy as jnp
from jax import lax
from jax.experimental import pallas as pl
from jax.experimental.pallas import tpu as pltpu
from jax.sharding import PartitionSpec as P

norm_eps = 1e-06
domain_scale = (1.0, 0.5, 2.0)
F32 = jnp.float32
BF16 = jnp.bfloat16
LANES = 128
VMEM_LIMIT = 56 * 1024 * 1024


def high_bit(s):
    return 1 << (s.bit_length() - 1)


def low_bit(s):
    return s & -s


def swap_dp(v, bit):
    return lax.ppermute(v, "dp", [(i, i ^ bit) for i in range(lax.axis_size("dp"))])


def swap_core(v):
    return lax.ppermute(v, "mp", [(i, i ^ 1) for i in range(lax.axis_size("mp"))])


def plane_gather(x):
    count = lax.axis_size("dp")
    half = x.shape[0] // 2
    first = {0: x[:half]}
    last = {0: x[half:]}
    for s in range(1, count):
        first[s] = swap_dp(first[s ^ high_bit(s)], high_bit(s))
        last[s] = swap_dp(last[s ^ low_bit(s)], low_bit(s))
    slots = []
    for s in range(count):
        own = x if s == 0 else jnp.concatenate([first[s], last[s]], 0)
        slots.append(jnp.concatenate([own, swap_core(own)], 0))
    return slots


def bit_flip(s, bits):
    return int(format(s, "0" + str(bits) + "b")[::-1], 2)


def plane_scatter(parts):
    count = len(parts)
    bits = max(count.bit_length() - 1, 1)
    rows = parts[0].shape[0] // 2
    half = rows // 2
    first = {}
    last = {}
    for s in reversed(range(count)):
        both = parts[s][:rows].astype(F32) + swap_core(parts[s][rows:]).astype(F32)
        first[s] = both[:half]
        last[s] = both[half:]
    for s in reversed(range(1, count)):
        bit = high_bit(s)
        first[s ^ bit] = first[s ^ bit] + swap_dp(first[s].astype(BF16), bit).astype(F32)
    for s in sorted(range(1, count), key=lambda s: -bit_flip(s, bits)):
        bit = low_bit(s)
        last[s ^ bit] = last[s ^ bit] + swap_dp(last[s].astype(BF16), bit).astype(F32)
    return jnp.concatenate([first[0], last[0]], 0)


def plane_scatter_rows(totals):
    part = totals[:, 0] + swap_core(totals[:, 1])
    while part.shape[0] > 1:
        half = part.shape[0] // 2
        part = part[:half] + swap_dp(part[half:], half)
    return part[0]


def plane_gather_rows(vec):
    part = jnp.stack([vec, swap_core(vec)], 0)[None]
    while part.shape[0] < lax.axis_size("dp"):
        part = jnp.concatenate([part, swap_dp(part, part.shape[0])], 0)
    return part.reshape(-1, vec.shape[0])


def line_groups():
    size = lax.axis_size("mp")
    return [[place * 2 + core for place in range(size // 2)] for core in (0, 1)]


def line_gather(v):
    return lax.all_gather(v, "mp", axis=0, tiled=False, axis_index_groups=line_groups())


def line_scatter(v):
    return lax.psum_scatter(
        v, "mp", scatter_dimension=0, tiled=False, axis_index_groups=line_groups()
    )


def line_carry(decay, value, ahead):
    size = lax.axis_size("mp")
    packed = jnp.stack([decay, value], 0)
    total = None
    for step in reversed(range(1, size // 2)):
        pairs = [(i, i + 2 * step) for i in range(size - 2 * step)]
        if ahead:
            pairs = [(b, a) for a, b in pairs]
        got = lax.ppermute(packed, "mp", pairs)
        total = got[1] if total is None else got[1] + got[0] * total
    return jnp.zeros_like(value) if total is None else total


def in_order(core, own, other):
    return jnp.where(core == 0, own, other), jnp.where(core == 0, other, own)


def scan_kernel(slots, core_ref, *refs):
    inputs, forgets, rest = refs[:slots], refs[slots : 2 * slots], refs[2 * slots :]
    bound_ref, local_ref, decay_ref, end_ref, full_ref, seq_end_ref, seq_full_ref = rest
    pair = inputs[0].shape[0]
    rows = pair // 2
    blocks = 2 * slots
    low = bound_ref[...]
    for s in range(slots):
        forget = low + (1.0 - low) * jax.nn.sigmoid(forgets[s][...])
        decay_ref[pl.ds(s * pair, pair), :] = forget
        local_ref[pl.ds(s * pair, pair), :] = (1.0 - forget) * jax.nn.silu(inputs[s][...])

    def step(t, kept):
        state, decay = kept
        place = pl.ds(t, blocks, stride=rows)
        forget = decay_ref[place, :]
        state = forget * state + local_ref[place, :]
        decay = forget * decay
        local_ref[place, :] = state
        decay_ref[place, :] = decay
        return state, decay

    none = decay_ref[pl.ds(0, blocks, stride=rows), :] * 0.0
    end, full = lax.fori_loop(0, rows, step, (none, none + 1.0), unroll=8)
    end_ref[...] = end
    full_ref[...] = full
    core = core_ref[0]
    own, other = pl.ds(0, slots, stride=2), pl.ds(1, slots, stride=2)
    end_a, end_b = in_order(core, end_ref[own, :], end_ref[other, :])
    full_a, full_b = in_order(core, full_ref[own, :], full_ref[other, :])
    seq_end_ref[...] = end_b + full_b * end_a
    seq_full_ref[...] = full_a * full_b


def state_kernel(slots, core_ref, *refs):
    gates, rest = refs[:slots], refs[slots:]
    local_ref, decay_ref, end_ref, full_ref, enter_ref, gain_ref = rest[:6]
    state_ref, square_ref, carry_ref = rest[6:9]
    outs = rest[9:]
    pair = gates[0].shape[0]
    rows = pair // 2
    core = core_ref[0]
    own, other = pl.ds(0, slots, stride=2), pl.ds(1, slots, stride=2)
    end_a, _ = in_order(core, end_ref[own, :], end_ref[other, :])
    full_a, _ = in_order(core, full_ref[own, :], full_ref[other, :])
    carry_a = enter_ref[...]
    carry_b = end_a + full_a * carry_a
    carry_own, carry_other = in_order(core, carry_a, carry_b)
    carry_ref[own, :] = carry_own
    carry_ref[other, :] = carry_other
    gain = gain_ref[...]
    for s in range(slots):
        for side in (0, 1):
            block = 2 * s + side
            here = pl.ds(block * rows, rows)
            state = local_ref[here, :] + decay_ref[here, :] * carry_ref[block : block + 1, :]
            state_ref[here, :] = state
            gated = state * jax.nn.silu(gates[s][pl.ds(side * rows, rows), :])
            outs[s][pl.ds(side * rows, rows), :] = (gated * gain).astype(BF16)
            total = jnp.sum((gated * gated).T, 0, keepdims=True)

            @pl.when(pl.program_id(0) == 0)
            def _(block=block, total=total):
                square_ref[block : block + 1, :] = total

            @pl.when(pl.program_id(0) > 0)
            def _(block=block, total=total):
                square_ref[block : block + 1, :] = square_ref[block : block + 1, :] + total


def across(row, lanes):
    return jnp.broadcast_to(row, (lanes, row.shape[1])).T


def scan_back_kernel(slots, core_ref, *refs):
    grads, forgets, gates, rest = (
        refs[:slots],
        refs[slots : 2 * slots],
        refs[2 * slots : 3 * slots],
        refs[3 * slots :],
    )
    state_ref, stat_ref, bound_ref, gain_ref = rest[:4]
    local_ref, decay_ref, end_ref, full_ref, seq_end_ref, seq_full_ref = rest[4:10]
    (forget_ref,) = rest[10:]
    pair = grads[0].shape[0]
    rows = pair // 2
    blocks = 2 * slots
    low = bound_ref[...]
    gain = gain_ref[...]
    for s in range(slots):
        for side in (0, 1):
            block = 2 * s + side
            here, part = pl.ds(block * rows, rows), pl.ds(side * rows, rows)
            silu_gate = jax.nn.silu(gates[s][part, :])
            gated = state_ref[here, :] * silu_gate
            dgated = grads[s][part, :] * gain - gated * across(
                stat_ref[block : block + 1, :], LANES
            )
            local_ref[here, :] = dgated * silu_gate
            forget_ref[here, :] = low + (1.0 - low) * jax.nn.sigmoid(forgets[s][part, :])

    def step(k, kept):
        t = rows - 1 - k
        state, decay, forget = kept
        place = pl.ds(t, blocks, stride=rows)
        state = forget * state + local_ref[place, :]
        decay = forget * decay
        local_ref[place, :] = state
        decay_ref[place, :] = decay
        return state, decay, forget_ref[place, :]

    none = forget_ref[pl.ds(0, blocks, stride=rows), :] * 0.0
    state, decay, forget = lax.fori_loop(
        0, rows, step, (none, none + 1.0, none + 1.0), unroll=8
    )
    end_ref[...] = forget * state
    full_ref[...] = forget * decay
    core = core_ref[0]
    own, other = pl.ds(0, slots, stride=2), pl.ds(1, slots, stride=2)
    end_a, end_b = in_order(core, end_ref[own, :], end_ref[other, :])
    full_a, full_b = in_order(core, full_ref[own, :], full_ref[other, :])
    seq_end_ref[...] = end_a + full_a * end_b
    seq_full_ref[...] = full_a * full_b


def project_back_kernel(slots, core_ref, *refs):
    grads, inputs, forgets, gates, rest = (
        refs[:slots],
        refs[slots : 2 * slots],
        refs[2 * slots : 3 * slots],
        refs[3 * slots : 4 * slots],
        refs[4 * slots :],
    )
    state_ref, stat_ref, bound_ref, gain_ref, carry_ref = rest[:5]
    local_ref, decay_ref, end_ref, full_ref, enter_ref = rest[5:10]
    out_ref, bound_grad_ref, gain_grad_ref, back_ref = rest[10:]
    pair = grads[0].shape[0]
    rows = pair // 2
    core = core_ref[0]
    width = out_ref.shape[1] // 3
    column = pl.program_id(0) * LANES
    own, other = pl.ds(0, slots, stride=2), pl.ds(1, slots, stride=2)
    _, end_b = in_order(core, end_ref[own, :], end_ref[other, :])
    _, full_b = in_order(core, full_ref[own, :], full_ref[other, :])
    carry_b = enter_ref[...]
    carry_a = end_b + full_b * carry_b
    carry_own, carry_other = in_order(core, carry_a, carry_b)
    back_ref[own, :] = carry_own
    back_ref[other, :] = carry_other
    low = bound_ref[...]
    gain = gain_ref[...]
    bound_total = jnp.zeros((1, LANES), F32)
    gain_total = jnp.zeros((1, LANES), F32)
    top = lax.broadcasted_iota(jnp.int32, (rows, LANES), 0) == 0
    for s in range(slots):
        for side in (0, 1):
            block = 2 * s + side
            here, part = pl.ds(block * rows, rows), pl.ds(side * rows, rows)
            state = state_ref[here, :]
            before = jnp.where(top, carry_ref[block : block + 1, :], pltpu.roll(state, 1, 0))
            gate = gates[s][part, :]
            gate_sig = jax.nn.sigmoid(gate)
            silu_gate = gate * gate_sig
            grad = grads[s][part, :]
            gated = state * silu_gate
            dgated = grad * gain - gated * across(stat_ref[block : block + 1, :], LANES)
            dstate = local_ref[here, :] + decay_ref[here, :] * back_ref[block : block + 1, :]
            enter = inputs[s][part, :]
            enter_sig = jax.nn.sigmoid(enter)
            forget_sig = jax.nn.sigmoid(forgets[s][part, :])
            keep = (1.0 - low) * (1.0 - forget_sig)
            dforget = dstate * (before - enter * enter_sig)
            slope = dforget * (1.0 - forget_sig)
            dinput = dstate * keep * enter_sig * (1.0 + enter * (1.0 - enter_sig))
            dpre = slope * (1.0 - low) * forget_sig
            dgate = dgated * state * gate_sig * (1.0 + gate * (1.0 - gate_sig))
            out_ref[here, pl.ds(pl.multiple_of(column, LANES), LANES)] = dinput.astype(BF16)
            out_ref[here, pl.ds(pl.multiple_of(width + column, LANES), LANES)] = dpre.astype(BF16)
            out_ref[here, pl.ds(pl.multiple_of(2 * width + column, LANES), LANES)] = dgate.astype(
                BF16
            )
            bound_total = bound_total + jnp.sum(slope, 0, keepdims=True)
            gain_total = gain_total + jnp.sum(grad * gated, 0, keepdims=True)
    bound_grad_ref[...] = bound_total
    gain_grad_ref[...] = gain_total


def column_block(rows, offset=0):
    return pl.BlockSpec((rows, LANES), lambda i, offset=offset: (0, offset + i))


def kernel_call(body, name, steps, in_specs, out_specs, out_shapes, scratch, flops, args):
    moved = sum(a.size * a.dtype.itemsize for a in args)
    moved += sum(s.size * s.dtype.itemsize for s in out_shapes)
    return pl.pallas_call(
        body,
        name=name,
        grid=(steps,),
        in_specs=[pl.BlockSpec(memory_space=pltpu.SMEM)] + in_specs,
        out_specs=out_specs,
        out_shape=out_shapes,
        scratch_shapes=scratch,
        compiler_params=pltpu.CompilerParams(
            vmem_limit_bytes=VMEM_LIMIT, dimension_semantics=("arbitrary",)
        ),
        cost_estimate=pl.CostEstimate(flops=flops, bytes_accessed=moved, transcendentals=0),
    )(*args)


def struct(shape, dtype=F32):
    return jax.ShapeDtypeStruct(shape, dtype)


def mixer_scan(core, projected, bound):
    slots = len(projected)
    pair = projected[0].shape[0]
    channels = projected[0].shape[1] // 3
    steps = channels // LANES
    total = pair * slots
    return kernel_call(
        functools.partial(scan_kernel, slots),
        "mixer_scan",
        steps,
        [column_block(pair)] * slots + [column_block(pair, steps)] * slots + [column_block(1)],
        [column_block(total)] * 2 + [column_block(2 * slots)] * 2 + [column_block(slots)] * 2,
        [struct((total, channels))] * 2
        + [struct((2 * slots, channels))] * 2
        + [struct((slots, channels))] * 2,
        [],
        total * channels * 200,
        [core] + projected + projected + [bound],
    )


def mixer_state(core, projected, local, decay, end, full, enter, gain):
    slots = len(projected)
    pair = projected[0].shape[0]
    channels = projected[0].shape[1] // 3
    steps = channels // LANES
    total = pair * slots
    outs = kernel_call(
        functools.partial(state_kernel, slots),
        "mixer_state",
        steps,
        [column_block(pair, 2 * steps)] * slots
        + [column_block(total)] * 2
        + [column_block(2 * slots)] * 2
        + [column_block(slots), column_block(1)],
        [
            column_block(total),
            pl.BlockSpec((2 * slots, pair // 2), lambda i: (0, 0)),
            column_block(2 * slots),
        ]
        + [column_block(pair)] * slots,
        [
            struct((total, channels)),
            struct((2 * slots, pair // 2)),
            struct((2 * slots, channels)),
        ]
        + [struct((pair, channels), BF16)] * slots,
        [],
        total * channels * 100,
        [core] + projected + [local, decay, end, full, enter, gain],
    )
    return outs[0], outs[1], outs[2], list(outs[3:])


def mixer_scan_back(core, grads, projected, state, stat, bound, gain):
    slots = len(projected)
    pair = projected[0].shape[0]
    channels = projected[0].shape[1] // 3
    steps = channels // LANES
    total = pair * slots
    return kernel_call(
        functools.partial(scan_back_kernel, slots),
        "mixer_scan_back",
        steps,
        [column_block(pair)] * slots
        + [column_block(pair, steps)] * slots
        + [column_block(pair, 2 * steps)] * slots
        + [column_block(total)]
        + [pl.BlockSpec((2 * slots, pair // 2), lambda i: (0, 0))]
        + [column_block(1)] * 2,
        [column_block(total)] * 2 + [column_block(2 * slots)] * 2 + [column_block(slots)] * 2,
        [struct((total, channels))] * 2
        + [struct((2 * slots, channels))] * 2
        + [struct((slots, channels))] * 2,
        [pltpu.VMEM((total, LANES), F32)],
        total * channels * 200,
        [core] + grads + projected + projected + [state, stat, bound, gain],
    )


def mixer_project_back(
    core, grads, projected, state, stat, bound, gain, carry, local, decay, end, full, enter
):
    slots = len(projected)
    pair = projected[0].shape[0]
    channels = projected[0].shape[1] // 3
    steps = channels // LANES
    total = pair * slots
    return kernel_call(
        functools.partial(project_back_kernel, slots),
        "mixer_project_back",
        steps,
        [column_block(pair)] * slots
        + [column_block(pair)] * slots
        + [column_block(pair, steps)] * slots
        + [column_block(pair, 2 * steps)] * slots
        + [column_block(total)]
        + [pl.BlockSpec((2 * slots, pair // 2), lambda i: (0, 0))]
        + [column_block(1)] * 2
        + [column_block(2 * slots)]
        + [column_block(total)] * 2
        + [column_block(2 * slots)] * 2
        + [column_block(slots)],
        [pl.BlockSpec((total, 3 * channels), lambda i: (0, 0))] + [column_block(1)] * 2,
        [struct((total, 3 * channels), BF16)] + [struct((1, channels))] * 2,
        [pltpu.VMEM((2 * slots, LANES), F32)],
        total * channels * 200,
        [core]
        + grads
        + projected * 3
        + [state, stat, bound, gain, carry, local, decay, end, full, enter],
    )


def matmul(a, b):
    return jnp.dot(a, b, preferred_element_type=F32)


def matmul_t(a, b):
    return lax.dot_general(a, b, (((1,), (1,)), ((), ())), preferred_element_type=F32)


def matmul_rows(a, b):
    return lax.dot_general(a, b, (((0,), (0,)), ((), ())), preferred_element_type=F32)


def rms_factor(values):
    return lax.rsqrt(jnp.mean(values * values, -1, keepdims=True) + norm_eps)


def rms_back(values, gain, grad):
    factor = rms_factor(values)
    normed = values * factor
    scaled = grad * gain
    back = factor * (scaled - normed * jnp.mean(scaled * normed, -1, keepdims=True))
    return back, jnp.sum(grad * normed, 0)


def bound_rows(logits):
    return jnp.cumsum(jax.nn.softmax(logits, 0), 0)


def local(
    hidden_in,
    cotangent,
    domain_tags,
    mix_weight,
    mix_out_weight,
    glu_weight,
    glu_out_weight,
    mix_gain,
    out_gain,
    glu_gain,
    bound_logits,
):
    dp = lax.axis_size("dp")
    line = lax.axis_size("mp") // 2
    column = lax.axis_index("dp")
    member = lax.axis_index("mp")
    core = member % 2
    core_arg = core.astype(jnp.int32).reshape(1)
    width = hidden_in.shape[1]
    layers = mix_weight.shape[0]
    channels = mix_weight.shape[3]
    units = glu_weight.shape[3]
    c_strip, u_strip = channels // dp, units // dp

    def cut(array, axis, size):
        return lax.dynamic_slice_in_dim(array, column * size, size, axis)

    mix_w, out_w, gate_w, up_w, down_w = [], [], [], [], []
    for l in range(layers):
        mix_strip = cut(mix_weight[l], 2, c_strip).transpose(1, 2, 0).reshape(3 * c_strip, width)
        out_strip = cut(mix_out_weight[l], 0, c_strip)
        glu_strip = cut(glu_weight[l], 2, u_strip).transpose(1, 2, 0).reshape(2 * u_strip, width)
        down_strip = cut(glu_out_weight[l], 0, u_strip)
        got = line_gather(mix_strip).reshape(line, 3, c_strip, width)
        mix_w.append(got.transpose(1, 0, 2, 3).reshape(3 * line * c_strip, width))
        got = line_gather(jnp.concatenate([out_strip, glu_strip, down_strip], 0))
        out_w.append(got[:, :c_strip].reshape(line * c_strip, width))
        start = c_strip
        gate_w.append(got[:, start : start + u_strip].reshape(line * u_strip, width))
        start += u_strip
        up_w.append(got[:, start : start + u_strip].reshape(line * u_strip, width))
        start += u_strip
        down_w.append(got[:, start : start + u_strip].reshape(line * u_strip, width))
    bound_vals, bound_back = jax.vjp(bound_rows, bound_logits)
    small = jnp.concatenate([cut(bound_vals, 1, c_strip), cut(out_gain, 1, c_strip)], 0)
    small = line_gather(small).transpose(1, 0, 2).reshape(-1, line * c_strip)
    bounds = [small[l : l + 1] for l in range(layers)]
    gains = [small[bound_vals.shape[0] + l :][:1] for l in range(layers)]

    stream = hidden_in.astype(F32)
    kept = []
    for l in range(layers):
        stream_in = stream
        mixer_in = plane_gather((stream * rms_factor(stream) * mix_gain[l]).astype(BF16))
        projected = [matmul_t(rows, mix_w[l]) for rows in mixer_in]
        scanned, decay, end, full, seq_end, seq_full = mixer_scan(core_arg, projected, bounds[l])
        enter = line_carry(seq_full, seq_end, False)
        state, squares, carry, mixed = mixer_state(
            core_arg, projected, scanned, decay, end, full, enter, gains[l]
        )
        parts = [matmul(rows, out_w[l]).astype(BF16) for rows in mixed]
        total = plane_scatter_rows(squares.reshape(dp, 2, -1))
        out_factor = lax.rsqrt(total / width + norm_eps)[:, None]
        raw = plane_scatter(parts)
        stream_mid = stream + raw * out_factor
        glu_in = plane_gather((stream_mid * rms_factor(stream_mid) * glu_gain[l]).astype(BF16))
        gate = [matmul_t(rows, gate_w[l]) for rows in glu_in]
        up = [matmul_t(rows, up_w[l]) for rows in glu_in]
        hidden = [(jax.nn.silu(a) * b).astype(BF16) for a, b in zip(gate, up)]
        parts = [matmul(rows, down_w[l]).astype(BF16) for rows in hidden]
        stream = stream_mid + plane_scatter(parts)
        kept.append(
            (
                stream_in,
                mixer_in,
                projected,
                state,
                carry,
                mixed,
                out_factor,
                raw,
                stream_mid,
                glu_in,
                gate,
                up,
                hidden,
            )
        )

    scale_table = jnp.array(domain_scale, dtype=F32)
    match = domain_tags[0] == jnp.arange(3, dtype=jnp.int32)
    grad = cotangent.astype(F32) * jnp.sum(jnp.where(match, scale_table, 0.0))
    mix_grads = [None] * layers
    mix_out_grads = [None] * layers
    glu_grads = [None] * layers
    glu_out_grads = [None] * layers
    mix_gain_parts = [None] * layers
    glu_gain_parts = [None] * layers
    out_gain_parts = [None] * layers
    bound_parts = [None] * layers
    for l in reversed(range(layers)):
        (
            stream_in,
            mixer_in,
            projected,
            state,
            carry,
            mixed,
            out_factor,
            raw,
            stream_mid,
            glu_in,
            gate,
            up,
            hidden,
        ) = kept[l]
        down_grad = plane_gather(grad.astype(BF16))
        parts, dgates, dups = [], [], []
        for s in range(dp):
            dhidden = matmul_t(down_grad[s], down_w[l])
            sig = jax.nn.sigmoid(gate[s])
            dgates.append((dhidden * up[s] * sig * (1.0 + gate[s] * (1.0 - sig))).astype(BF16))
            dups.append((dhidden * gate[s] * sig).astype(BF16))
            parts.append((matmul(dgates[s], gate_w[l]) + matmul(dups[s], up_w[l])).astype(BF16))
        back, glu_gain_parts[l] = rms_back(stream_mid, glu_gain[l], plane_scatter(parts))
        glu_rows = jnp.concatenate(glu_in, 0)
        down_part = matmul_rows(jnp.concatenate(hidden, 0), jnp.concatenate(down_grad, 0))
        gate_part = matmul_rows(jnp.concatenate(dgates, 0), glu_rows)
        up_part = matmul_rows(jnp.concatenate(dups, 0), glu_rows)
        sent = jnp.concatenate(
            [v.astype(BF16).reshape(line, u_strip, width) for v in (down_part, gate_part, up_part)],
            1,
        )
        strips = lax.all_gather(line_scatter(sent), "dp", axis=0)
        glu_out_grads[l] = strips[:, :u_strip].reshape(units, width).astype(F32)
        glu_grads[l] = (
            strips[:, u_strip:]
            .reshape(dp, 2, u_strip, width)
            .transpose(3, 1, 0, 2)
            .reshape(width, 2, units)
            .astype(F32)
        )
        grad = grad + back

        out_low = (grad * out_factor).astype(BF16)
        stat = jnp.mean(out_low.astype(F32) * raw, -1) * (out_factor * out_factor)[:, 0]
        stats = plane_gather_rows(stat)
        out_grad = plane_gather(out_low)
        mixed_grad = [matmul_t(rows, out_w[l]) for rows in out_grad]
        scanned, decay, end, full, seq_end, seq_full = mixer_scan_back(
            core_arg, mixed_grad, projected, state, stats, bounds[l], gains[l]
        )
        enter = line_carry(seq_full, seq_end, True)
        proj_grad, bound_parts[l], out_gain_parts[l] = mixer_project_back(
            core_arg,
            mixed_grad,
            projected,
            state,
            stats,
            bounds[l],
            gains[l],
            carry,
            scanned,
            decay,
            end,
            full,
            enter,
        )
        pair = projected[0].shape[0]
        parts = [
            matmul(proj_grad[s * pair : (s + 1) * pair], mix_w[l]).astype(BF16) for s in range(dp)
        ]
        mix_part = matmul_rows(proj_grad, jnp.concatenate(mixer_in, 0))
        out_part = matmul_rows(jnp.concatenate(mixed, 0), jnp.concatenate(out_grad, 0))
        mix_sent = mix_part.astype(BF16).reshape(3, line, c_strip, width).transpose(1, 0, 2, 3)
        sent = jnp.concatenate(
            [
                mix_sent.reshape(line, 3 * c_strip, width),
                out_part.astype(BF16).reshape(line, c_strip, width),
            ],
            1,
        )
        strips = lax.all_gather(line_scatter(sent), "dp", axis=0)
        mix_out_grads[l] = strips[:, 3 * c_strip :].reshape(channels, width).astype(F32)
        mix_grads[l] = (
            strips[:, : 3 * c_strip]
            .reshape(dp, 3, c_strip, width)
            .transpose(3, 1, 0, 2)
            .reshape(width, 3, channels)
            .astype(F32)
        )
        back, mix_gain_parts[l] = rms_back(stream_in, mix_gain[l], plane_scatter(parts))
        grad = grad + back

    def spread(row):
        zeros = jnp.zeros((line, 2, dp, c_strip), F32)
        return lax.dynamic_update_slice(
            zeros, row.reshape(line, 1, 1, c_strip), (0, core, column, 0)
        ).reshape(-1)

    rows = jnp.stack(
        mix_gain_parts
        + glu_gain_parts
        + [spread(v) for v in out_gain_parts]
        + [spread(v) for v in bound_parts]
    )
    rows = lax.psum(rows, ("dp", "mp"))
    mix_gain_grad = rows[:layers]
    glu_gain_grad = rows[layers : 2 * layers]
    mine = lax.dynamic_slice_in_dim(rows[2 * layers :], member * channels, channels, 1)
    out_gain_grad = mine[:layers]
    extra = jnp.zeros((bound_vals.shape[0] - layers, channels), F32)
    bound_grad = bound_back(jnp.concatenate([mine[layers:], extra], 0))[0]
    return (
        stream,
        grad,
        jnp.stack(mix_grads),
        jnp.stack(mix_out_grads),
        jnp.stack(glu_grads),
        jnp.stack(glu_out_grads),
        mix_gain_grad,
        out_gain_grad,
        glu_gain_grad,
        bound_grad,
    )


def solution(mesh):
    return jax.shard_map(
        local,
        mesh=mesh,
        in_specs=(
            P(("dp", "mp"), None),
            P(("dp", "mp"), None),
            P("dp"),
            P(None, None, None, "mp"),
            P(None, "mp", None),
            P(None, None, None, "mp"),
            P(None, "mp", None),
            P(),
            P(None, "mp"),
            P(),
            P(None, "mp"),
        ),
        out_specs=(
            P(("dp", "mp"), None),
            P(("dp", "mp"), None),
            P(None, None, None, "mp"),
            P(None, "mp", None),
            P(None, None, None, "mp"),
            P(None, "mp", None),
            P(),
            P(None, "mp"),
            P(),
            P(None, "mp"),
        ),
        check_vma=False,
    )
```

```python
import functools

import jax
import jax.numpy as jnp
from jax import lax
from jax.experimental import pallas as pl
from jax.experimental.pallas import tpu as pltpu
from jax.sharding import PartitionSpec as P

norm_eps = 1e-06
domain_scale = (1.0, 0.5, 2.0)
F32 = jnp.float32
BF16 = jnp.bfloat16
LANES = 128
VMEM_LIMIT = 56 * 1024 * 1024


def high_bit(s):
    return 1 << (s.bit_length() - 1)


def low_bit(s):
    return s & -s


def swap_dp(v, bit):
    return lax.ppermute(v, "dp", [(i, i ^ bit) for i in range(lax.axis_size("dp"))])


def swap_core(v):
    return lax.ppermute(v, "mp", [(i, i ^ 1) for i in range(lax.axis_size("mp"))])


def slot_groups():
    slots = sorted(range(lax.axis_size("dp")), key=lambda s: (bin(s).count("1"), s))
    near = [s for s in slots if bin(s).count("1") <= 1]
    return near, slots[len(near) :]


def join(parts):
    return parts[0] if len(parts) == 1 else jnp.concatenate(parts, 0)


def plane_gather(x):
    near, far = slot_groups()
    half = x.shape[0] // 2
    slots = {0: x}
    for s in near[1:]:
        slots[s] = swap_dp(x, s)
    for s in far:
        top, low = high_bit(s), low_bit(s)
        slots[s] = join([swap_dp(slots[s ^ top][:half], top), swap_dp(slots[s ^ low][half:], low)])
    own = join([slots[s] for s in range(len(slots))])
    return [own, swap_core(own)]


def plane_scatter(own, other, product, first_fill=(), last_fill=()):
    near, far = slot_groups()
    count = own.shape[0] // lax.axis_size("dp")
    half = count // 2
    other = swap_core(product(other).astype(BF16))
    both = product(own) + other.astype(F32)
    total = {s: both[s * count : (s + 1) * count] for s in near + far}
    for s in reversed(far):
        top, low = high_bit(s), low_bit(s)
        first = swap_dp(total[s][:half].astype(BF16), top)
        last = swap_dp(total[s][half:].astype(BF16), low)
        if s == far[0]:
            first, last, first_fill = tie_all(first, last, first_fill)
        total[s ^ top] = join([total[s ^ top][:half] + first.astype(F32), total[s ^ top][half:]])
        total[s ^ low] = join([total[s ^ low][:half], total[s ^ low][half:] + last.astype(F32)])
    got = [swap_dp(total[s].astype(BF16), s) for s in near[1:]]
    got, last_fill = tie_all(got, last_fill)
    out = total[0]
    for v in got:
        out = out + v.astype(F32)
    return out, first_fill, last_fill


def plane_scatter_rows(totals):
    part = totals[:, 0] + swap_core(totals[:, 1])
    while part.shape[0] > 1:
        half = part.shape[0] // 2
        part = part[:half] + swap_dp(part[half:], half)
    return part[0]


def in_parts(vec):
    parts = []
    rest = vec
    for _ in range(3):
        part = lax.reduce_precision(rest, 8, 7)
        rest = rest - part
        parts.append(part.astype(BF16))
    return jnp.pad(jnp.stack(parts, 1), ((0, 0), (0, LANES - 3)))


def strip_halves(v):
    half = v.shape[1] // 32 * 16
    return v[0, :half], v[0, half:]


def strips_near(halves):
    near, _ = slot_groups()
    slots = {0: tuple(halves)}
    for s in near[1:]:
        slots[s] = tuple(swap_dp(v, s) for v in halves)
    return slots


def strips_far(slots):
    near, far = slot_groups()
    slots = dict(slots)
    for s in far:
        top, low = high_bit(s), low_bit(s)
        slots[s] = (swap_dp(slots[s ^ top][0], top), swap_dp(slots[s ^ low][1], low))
    return [slots[s] for s in range(len(slots))]


def in_columns(slots):
    slots = jnp.stack([jnp.concatenate(halves, 0) for halves in slots], 0)
    column = lax.axis_index("dp")
    return jnp.stack(
        [
            lax.dynamic_index_in_dim(slots, column ^ s, 0, keepdims=False)
            for s in range(slots.shape[0])
        ],
        0,
    )


def line_sum(v):
    size = lax.axis_size("mp")
    bit = 2
    while bit < size:
        v = v + lax.ppermute(v, "mp", [(i, i ^ bit) for i in range(size)])
        bit *= 2
    return v


def sum_all(v):
    v = v + swap_core(v)
    bit = 1
    while bit < lax.axis_size("dp"):
        v = v + swap_dp(v, bit)
        bit *= 2
    return line_sum(v)


def tie_all(*values):
    return lax.optimization_barrier(values)


def line_groups():
    size = lax.axis_size("mp")
    return [[place * 2 + core for place in range(size // 2)] for core in (0, 1)]


def line_gather(v):
    return lax.all_gather(v, "mp", axis=0, tiled=False, axis_index_groups=line_groups())


def line_scatter(v):
    return lax.psum_scatter(
        v, "mp", scatter_dimension=0, tiled=True, axis_index_groups=line_groups()
    )


def line_carry(decay, value, ahead):
    size = lax.axis_size("mp")
    packed = jnp.stack([decay, value], 0)
    total = None
    for step in reversed(range(1, size // 2)):
        pairs = [(i, i + 2 * step) for i in range(size - 2 * step)]
        if ahead:
            pairs = [(b, a) for a, b in pairs]
        got = lax.ppermute(packed, "mp", pairs)
        total = got[1] if total is None else got[1] + got[0] * total
    return jnp.zeros_like(value) if total is None else total


def in_order(core, own, other):
    return jnp.where(core == 0, own, other), jnp.where(core == 0, other, own)


def take(refs, count):
    return refs[:count], refs[count:]


class Places:
    def __init__(self, slots, rows):
        self.blocks, self.rows, self.half = 2 * slots, rows, rows // 2

    def __iter__(self):
        for block in range(self.blocks):
            for h in (0, 1):
                here = pl.ds(block * self.rows + h * self.half, self.half)
                part = pl.ds(block // 2 * self.half, self.half)
                yield block, h, here, 2 * h + block % 2, part


def scan_kernel(places, core_ref, *refs):
    pieces, rows = 4, places.rows
    inputs, refs = take(refs, pieces)
    forgets, refs = take(refs, pieces)
    bound_ref, local_ref, decay_ref, end_ref, full_ref, seq_end_ref, seq_full_ref = refs
    blocks = places.blocks
    low = bound_ref[...]
    for _, _, here, p, part in places:
        forget = low + (1.0 - low) * jax.nn.sigmoid(forgets[p][part, :])
        decay_ref[here, :] = forget
        local_ref[here, :] = (1.0 - forget) * jax.nn.silu(inputs[p][part, :])

    def step(t, kept):
        state, decay = kept
        place = pl.ds(t, blocks, stride=rows)
        forget = decay_ref[place, :]
        state = forget * state + local_ref[place, :]
        decay = forget * decay
        local_ref[place, :] = state
        decay_ref[place, :] = decay
        return state, decay

    none = decay_ref[pl.ds(0, blocks, stride=rows), :] * 0.0
    end, full = lax.fori_loop(0, rows, step, (none, none + 1.0), unroll=8)
    end_ref[...] = end
    full_ref[...] = full
    core = core_ref[0]
    own, other = pl.ds(0, blocks // 2, stride=2), pl.ds(1, blocks // 2, stride=2)
    end_a, end_b = in_order(core, end_ref[own, :], end_ref[other, :])
    full_a, full_b = in_order(core, full_ref[own, :], full_ref[other, :])
    seq_end_ref[...] = end_b + full_b * end_a
    seq_full_ref[...] = full_a * full_b


def state_kernel(places, core_ref, *refs):
    pieces = 4
    gates, refs = take(refs, pieces)
    local_ref, decay_ref, end_ref, full_ref, enter_ref, gain_ref = refs[:6]
    state_ref, square_ref, carry_ref = refs[6:9]
    outs = refs[9:]
    core = core_ref[0]
    slots = places.blocks // 2
    own, other = pl.ds(0, slots, stride=2), pl.ds(1, slots, stride=2)
    end_a, _ = in_order(core, end_ref[own, :], end_ref[other, :])
    full_a, _ = in_order(core, full_ref[own, :], full_ref[other, :])
    carry_a = enter_ref[...]
    carry_b = end_a + full_a * carry_a
    carry_own, carry_other = in_order(core, carry_a, carry_b)
    carry_ref[own, :] = carry_own
    carry_ref[other, :] = carry_other
    gain = gain_ref[...]
    for block, h, here, p, part in places:
        row = slice(block, block + 1)
        state = local_ref[here, :] + decay_ref[here, :] * carry_ref[row, :]
        state_ref[here, :] = state
        gated = state * jax.nn.silu(gates[p][part, :])
        outs[p][part, :] = (gated * gain).astype(BF16)
        total = jnp.sum((gated * gated).T, 0, keepdims=True)
        row = slice(h * places.blocks + block, h * places.blocks + block + 1)

        @pl.when(pl.program_id(0) == 0)
        def _(row=row, total=total):
            square_ref[row, :] = total

        @pl.when(pl.program_id(0) > 0)
        def _(row=row, total=total):
            square_ref[row, :] = square_ref[row, :] + total


def row_stat(parts):
    parts = parts.astype(F32)
    return (parts[:, 0:1] + parts[:, 1:2]) + parts[:, 2:3]


def scan_back_kernel(places, core_ref, *refs):
    pieces, rows = 4, places.rows
    grads, refs = take(refs, pieces)
    forgets, refs = take(refs, pieces)
    gates, refs = take(refs, pieces)
    stats, refs = take(refs, pieces)
    state_ref, bound_ref, gain_ref = refs[:3]
    local_ref, decay_ref, end_ref, full_ref, seq_end_ref, seq_full_ref, forget_ref = refs[3:]
    blocks = places.blocks
    low = bound_ref[...]
    gain = gain_ref[...]
    for _, _, here, p, part in places:
        silu_gate = jax.nn.silu(gates[p][part, :])
        gated = state_ref[here, :] * silu_gate
        stat = row_stat(stats[p][part, :])
        local_ref[here, :] = (grads[p][part, :] * gain - gated * stat) * silu_gate
        forget_ref[here, :] = low + (1.0 - low) * jax.nn.sigmoid(forgets[p][part, :])

    def step(k, kept):
        t = rows - 1 - k
        state, decay, forget = kept
        place = pl.ds(t, blocks, stride=rows)
        state = forget * state + local_ref[place, :]
        decay = forget * decay
        local_ref[place, :] = state
        decay_ref[place, :] = decay
        return state, decay, forget_ref[place, :]

    none = forget_ref[pl.ds(0, blocks, stride=rows), :] * 0.0
    state, decay, forget = lax.fori_loop(
        0, rows, step, (none, none + 1.0, none + 1.0), unroll=8
    )
    end_ref[...] = forget * state
    full_ref[...] = forget * decay
    core = core_ref[0]
    own, other = pl.ds(0, blocks // 2, stride=2), pl.ds(1, blocks // 2, stride=2)
    end_a, end_b = in_order(core, end_ref[own, :], end_ref[other, :])
    full_a, full_b = in_order(core, full_ref[own, :], full_ref[other, :])
    seq_end_ref[...] = end_a + full_a * end_b
    seq_full_ref[...] = full_a * full_b


def project_back_kernel(places, core_ref, *refs):
    pieces, half = 4, places.half
    grads, refs = take(refs, pieces)
    inputs, refs = take(refs, pieces)
    forgets, refs = take(refs, pieces)
    gates, refs = take(refs, pieces)
    stats, refs = take(refs, pieces)
    state_ref, bound_ref, gain_ref, carry_ref = refs[:4]
    local_ref, decay_ref, end_ref, full_ref, enter_ref = refs[4:9]
    outs, (bound_grad_ref, gain_grad_ref, back_ref) = take(refs[9:], pieces)
    core = core_ref[0]
    slots = places.blocks // 2
    width = outs[0].shape[1] // 3
    column = pl.program_id(0) * LANES
    own, other = pl.ds(0, slots, stride=2), pl.ds(1, slots, stride=2)
    _, end_b = in_order(core, end_ref[own, :], end_ref[other, :])
    _, full_b = in_order(core, full_ref[own, :], full_ref[other, :])
    carry_b = enter_ref[...]
    carry_a = end_b + full_b * carry_b
    carry_own, carry_other = in_order(core, carry_a, carry_b)
    back_ref[own, :] = carry_own
    back_ref[other, :] = carry_other
    low = bound_ref[...]
    gain = gain_ref[...]
    bound_total = jnp.zeros((1, LANES), F32)
    gain_total = jnp.zeros((1, LANES), F32)
    top = lax.broadcasted_iota(jnp.int32, (half, LANES), 0) == 0
    for block, h, here, p, part in places:
        row = slice(block, block + 1)
        state = state_ref[here, :]
        if h == 0:
            before = carry_ref[row, :]
        else:
            before = state_ref[pl.ds(block * places.rows + half - 1, 1), :]
        before = jnp.where(top, before, pltpu.roll(state, 1, 0))
        gate = gates[p][part, :]
        gate_sig = jax.nn.sigmoid(gate)
        silu_gate = gate * gate_sig
        grad = grads[p][part, :]
        gated = state * silu_gate
        dgated = grad * gain - gated * row_stat(stats[p][part, :])
        dstate = local_ref[here, :] + decay_ref[here, :] * back_ref[row, :]
        enter = inputs[p][part, :]
        enter_sig = jax.nn.sigmoid(enter)
        forget_sig = jax.nn.sigmoid(forgets[p][part, :])
        keep = (1.0 - low) * (1.0 - forget_sig)
        dforget = dstate * (before - enter * enter_sig)
        slope = dforget * (1.0 - forget_sig)
        made = (
            dstate * keep * enter_sig * (1.0 + enter * (1.0 - enter_sig)),
            slope * (1.0 - low) * forget_sig,
            dgated * state * gate_sig * (1.0 + gate * (1.0 - gate_sig)),
        )
        for which, value in enumerate(made):
            lanes = pl.ds(pl.multiple_of(which * width + column, LANES), LANES)
            outs[p][part, lanes] = value.astype(BF16)
        bound_total = bound_total + jnp.sum(slope, 0, keepdims=True)
        gain_total = gain_total + jnp.sum(grad * gated, 0, keepdims=True)
    bound_grad_ref[...] = bound_total
    gain_grad_ref[...] = gain_total


def struct(shape, dtype=F32):
    return jax.ShapeDtypeStruct(shape, dtype)


class Mixer:
    def __init__(self, core, projected, bound, gain):
        self.core, self.projected, self.bound, self.gain = core, projected, bound, gain
        self.total = sum(p.shape[0] for p in projected)
        self.blocks = 2 * lax.axis_size("dp")
        self.rows = self.total // self.blocks
        self.places = Places(lax.axis_size("dp"), self.rows)
        self.channels = projected[0].shape[1] // 3
        self.steps = self.channels // LANES

    def column(self, rows, offset=0):
        return pl.BlockSpec((rows, LANES), lambda i, offset=offset: (0, offset + i))

    def pieces(self, which=0):
        return [self.column(p.shape[0], which * self.steps) for p in self.projected]

    def whole(self, rows, columns):
        return pl.BlockSpec((rows, columns), lambda i: (0, 0))

    def scanned(self):
        sizes = [self.total] * 2 + [self.blocks] * 2 + [self.blocks // 2] * 2
        return [self.column(n) for n in sizes], [struct((n, self.channels)) for n in sizes]

    def call(self, body, name, in_specs, out_specs, out_shapes, scratch, flops, args):
        moved = 1024
        call = pl.pallas_call(
            functools.partial(body, self.places),
            name=name,
            grid=(self.steps,),
            in_specs=[pl.BlockSpec(memory_space=pltpu.SMEM)] + in_specs,
            out_specs=out_specs,
            out_shape=out_shapes,
            scratch_shapes=scratch,
            compiler_params=pltpu.CompilerParams(
                vmem_limit_bytes=VMEM_LIMIT, dimension_semantics=("arbitrary",)
            ),
            cost_estimate=pl.CostEstimate(
                flops=flops, bytes_accessed=moved, transcendentals=0
            ),
        )
        return list(call(self.core, *args))

    def scan(self):
        specs, shapes = self.scanned()
        return self.call(
            scan_kernel,
            "mixer_scan",
            self.pieces(0) + self.pieces(1) + [self.column(1)],
            specs,
            shapes,
            [],
            200,
            self.projected * 2 + [self.bound],
        )

    def state(self, scanned, enter):
        total, blocks, channels = self.total, self.blocks, self.channels
        sizes = [total] * 2 + [blocks] * 2 + [blocks // 2, 1]
        outs = self.call(
            state_kernel,
            "mixer_state",
            self.pieces(2) + [self.column(n) for n in sizes],
            [self.column(total), self.whole(2 * blocks, self.rows // 2), self.column(blocks)]
            + self.pieces(),
            [struct((total, channels)), struct((2 * blocks, self.rows // 2)), struct((blocks, channels))]
            + [struct((p.shape[0], channels), BF16) for p in self.projected],
            [],
            100,
            self.projected + scanned[:4] + [enter, self.gain],
        )
        return outs[0], outs[1], outs[2], list(outs[3:])

    def scan_back(self, grads, state, stats):
        specs, shapes = self.scanned()
        return self.call(
            scan_back_kernel,
            "mixer_scan_back",
            self.pieces()
            + self.pieces(1)
            + self.pieces(2)
            + [
                pl.BlockSpec((p.shape[0], LANES), lambda i, last=p.shape[1] // LANES - 1: (0, last))
                for p in stats
            ]
            + [self.column(self.total)]
            + [self.column(1)] * 2,
            specs,
            shapes,
            [pltpu.VMEM((self.total, LANES), F32)],
            250,
            grads + self.projected * 2 + stats + [state, self.bound, self.gain],
        )

    def project_back(self, grads, state, stats, carry, scanned, enter):
        total, blocks, channels = self.total, self.blocks, self.channels
        sizes = [1, 1, blocks, total, total, blocks, blocks, blocks // 2]
        outs = self.call(
            project_back_kernel,
            "mixer_project_back",
            self.pieces()
            + self.pieces(0)
            + self.pieces(1)
            + self.pieces(2)
            + [
                pl.BlockSpec((p.shape[0], LANES), lambda i, last=p.shape[1] // LANES - 1: (0, last))
                for p in stats
            ]
            + [self.column(total)]
            + [self.column(n) for n in sizes],
            [self.whole(*p.shape) for p in self.projected] + [self.column(1)] * 2,
            [struct(p.shape, BF16) for p in self.projected] + [struct((1, channels))] * 2,
            [pltpu.VMEM((blocks, LANES), F32)],
            200,
            grads
            + self.projected * 3
            + stats
            + [state, self.bound, self.gain, carry]
            + scanned[:4]
            + [enter],
        )
        return list(outs[:-2]), outs[-2], outs[-1]


def matmul(a, b):
    return jnp.dot(a, b, preferred_element_type=F32)


def matmul_t(a, b):
    return lax.dot_general(a, b, (((1,), (1,)), ((), ())), preferred_element_type=F32)


def matmul_rows(a, b):
    return lax.dot_general(a, b, (((0,), (0,)), ((), ())), preferred_element_type=F32)


def rows_product(a, b):
    return matmul_rows(join(a), join(b)).astype(BF16)


@jax.tree_util.register_pytree_node_class
class Pair:
    def __init__(self, a, b):
        self.a, self.b = a, b

    @property
    def shape(self):
        return self.a.shape

    def __getitem__(self, part):
        return Pair(self.a[part], self.b[part])

    def tree_flatten(self):
        return (self.a, self.b), None

    @classmethod
    def tree_unflatten(cls, _, parts):
        return cls(*parts)


def rms_factor(values):
    return lax.rsqrt(jnp.mean(values * values, -1, keepdims=True) + norm_eps)


def rms_back(values, gain, grad):
    factor = rms_factor(values)
    normed = values * factor
    scaled = grad * gain
    back = factor * (scaled - normed * jnp.mean(scaled * normed, -1, keepdims=True))
    return back, jnp.sum(grad * normed, 0)


def bound_rows(logits):
    return jnp.cumsum(jax.nn.softmax(logits, 0), 0)


def local(
    hidden_in,
    cotangent,
    domain_tags,
    mix_weight,
    mix_out_weight,
    glu_weight,
    glu_out_weight,
    mix_gain,
    out_gain,
    glu_gain,
    bound_logits,
):
    dp = lax.axis_size("dp")
    line = lax.axis_size("mp") // 2
    column = lax.axis_index("dp")
    member = lax.axis_index("mp")
    core = member % 2
    core_arg = core.astype(jnp.int32).reshape(1)
    width = hidden_in.shape[1]
    layers = mix_weight.shape[0]
    channels = mix_weight.shape[3]
    units = glu_weight.shape[3]
    c_strip, u_strip = channels // dp, units // dp

    def cut(array, axis, size):
        return lax.dynamic_slice_in_dim(array, column * size, size, axis)

    scale_table = jnp.array(domain_scale, dtype=F32)
    match = domain_tags[0] == jnp.arange(3, dtype=jnp.int32)
    grad = cotangent.astype(F32) * jnp.sum(jnp.where(match, scale_table, 0.0))
    bound_vals, bound_back = jax.vjp(bound_rows, bound_logits)

    mix_w, out_w, gate_w, up_w, down_w = ([None] * layers for _ in range(5))

    def mix_strip(weight, out=None):
        strip = cut(weight, 2, c_strip).transpose(1, 2, 0).reshape(3 * c_strip, width)
        return strip if out is None else jnp.concatenate([strip, cut(out, 0, c_strip)], 0)

    def glu_strip(weight):
        return cut(weight, 2, u_strip).transpose(1, 2, 0).reshape(2 * u_strip, width)

    def gather_mix(l, strip, out=None):
        got = line_gather(strip)
        mixes = got[:, : 3 * c_strip].reshape(line, 3, c_strip, width).transpose(1, 0, 2, 3)
        mix_w[l] = mixes.reshape(3 * line * c_strip, width)
        out = got[:, 3 * c_strip :] if out is None else line_gather(out)
        out_w[l] = out.reshape(line * c_strip, width)

    def gather_glu(l, strip):
        got = line_gather(strip)
        gate_w[l] = got[:, :u_strip].reshape(line * u_strip, width)
        up_w[l] = got[:, u_strip:].reshape(line * u_strip, width)

    def gather_down(l, strip):
        down_w[l] = line_gather(strip).reshape(line * u_strip, width)

    strip = mix_strip(mix_weight[0])
    strip, hidden_in, out_strip = tie_all(strip, hidden_in, mix_out_weight[0])
    gather_mix(0, strip, cut(out_strip, 0, c_strip))
    half = hidden_in.shape[0] // 2

    def halves(rows):
        return [rows[:half], rows[half:]]

    def gathered(lows):
        return [piece for low in lows for piece in plane_gather(low)]

    def normed(rows, gain):
        return (rows * rms_factor(rows) * gain).astype(BF16)

    grad = halves(grad)
    stream = halves(hidden_in.astype(F32))
    kept = []
    for l in range(layers):
        stream_in = stream
        lows = [normed(rows, mix_gain[l]) for rows in stream]
        if l == 0:
            small = jnp.concatenate([cut(bound_vals, 1, c_strip), cut(out_gain, 1, c_strip)], 0)
            lows, small, first_glu = tie_all(lows, small, glu_weight[0])
            strip, down = tie_all(glu_strip(first_glu), glu_out_weight[0])
            gather_glu(0, strip)
            down_strip = cut(down, 0, u_strip)
            small = lax.dynamic_update_slice(
                jnp.zeros((small.shape[0], line, c_strip), F32), small[:, None], (0, member // 2, 0)
            )
            small = line_sum(small).reshape(-1, line * c_strip)
            bounds = [small[i : i + 1] for i in range(layers)]
            gains = [small[bound_vals.shape[0] + i :][:1] for i in range(layers)]
        mixer_in = gathered(lows)
        projected = [matmul_t(rows, mix_w[l]) for rows in mixer_in]
        mixer = Mixer(core_arg, projected, bounds[l], gains[l])
        scanned = mixer.scan()
        enter = line_carry(scanned[5], scanned[4], False)
        state, squares, carry, mixed = mixer.state(scanned, enter)
        if l + 1 < layers:
            down_strip, *raws = tie_all(
                down_strip, mix_weight[l + 1], mix_out_weight[l + 1], glu_weight[l + 1]
            )
            gather_down(l, down_strip)
            strip, raw = tie_all(mix_strip(*raws[:2]), raws[2])
            gather_mix(l + 1, strip)
            strip, down = tie_all(glu_strip(raw), glu_out_weight[l + 1])
            gather_glu(l + 1, strip)
            down_strip = cut(down, 0, u_strip)
        else:
            gather_down(l, down_strip)
        squares = plane_scatter_rows(
            squares.reshape(2, dp, 2, half).transpose(1, 2, 0, 3).reshape(dp, 2, 2 * half)
        )
        out_factor = halves(lax.rsqrt(squares / width + norm_eps)[:, None])
        raw = [
            plane_scatter(*mixed[2 * h : 2 * h + 2], lambda rows, w=out_w[l]: matmul(rows, w))[0]
            for h in (0, 1)
        ]
        stream_mid = [a + b * c for a, b, c in zip(stream, raw, out_factor)]
        glu_in = gathered([normed(rows, glu_gain[l]) for rows in stream_mid])

        def glu(rows):
            a, b = matmul_t(rows, gate_w[l]), matmul_t(rows, up_w[l])
            return a, b, (jax.nn.silu(a) * b).astype(BF16)

        if l == 0:
            glu_in, grad_low = tie_all(glu_in, [rows.astype(BF16) for rows in grad])
            last_grad = gathered(grad_low)
        gate, up, hidden = zip(*[glu(rows) for rows in glu_in])
        if l == 0:
            hidden, last_grad = tie_all(hidden, last_grad)
        stream = [
            stream_mid[h]
            + plane_scatter(*hidden[2 * h : 2 * h + 2], lambda rows, w=down_w[l]: matmul(rows, w))[0]
            for h in (0, 1)
        ]
        kept.append(
            (
                stream_in,
                mixer_in,
                mixer,
                state,
                carry,
                mixed,
                out_factor,
                raw,
                stream_mid,
                glu_in,
                gate,
                up,
                hidden,
            )
        )

    mix_gain_parts = [None] * layers
    glu_gain_parts = [None] * layers
    out_gain_parts = [None] * layers
    bound_parts = [None] * layers

    grads = {}

    def place(name, l, value):
        if name not in grads:
            grads[name] = jnp.zeros((layers,) + value.shape, F32)
        grads[name] = lax.dynamic_update_index_in_dim(grads[name], value.astype(F32), l, 0)

    def finish_glu(l, slots):
        strips = in_columns(slots)
        place("glu_out", l, strips[:, :u_strip].reshape(units, width))
        strips = strips[:, u_strip:].reshape(dp, 2, u_strip, width).transpose(3, 1, 0, 2)
        place("glu", l, strips.reshape(width, 2, units))

    def finish_mix(l, slots):
        strips = in_columns(slots)
        place("mix_out", l, strips[:, 3 * c_strip :].reshape(channels, width))
        strips = strips[:, : 3 * c_strip].reshape(dp, 3, c_strip, width).transpose(3, 1, 0, 2)
        place("mix", l, strips.reshape(width, 3, channels))

    for l in reversed(range(layers)):
        (
            stream_in,
            mixer_in,
            mixer,
            state,
            carry,
            mixed,
            out_factor,
            raw,
            stream_mid,
            glu_in,
            gate,
            up,
            hidden,
        ) = kept[l]
        if l == layers - 1:
            down_grad = last_grad
        else:
            down_grad = gathered([rows.astype(BF16) for rows in grad])
            down_grad, glu_sum = tie_all(down_grad, glu_sum)
            glu_strips = strips_near(glu_sum)

        def glu_back(rows, a, b):
            dhidden = matmul_t(rows, down_w[l])
            sig = jax.nn.sigmoid(a)
            dgate = (dhidden * b * sig * (1.0 + a * (1.0 - sig))).astype(BF16)
            return Pair(dgate, (dhidden * a * sig).astype(BF16))

        def glu_product(rows):
            return matmul(rows.a, gate_w[l]) + matmul(rows.b, up_w[l])

        pairs = [glu_back(*args) for args in zip(down_grad, gate, up)]
        back_first, _, _ = plane_scatter(*pairs[:2], glu_product)
        fill = (
            rows_product([p.a for p in pairs], glu_in),
            rows_product([p.b for p in pairs], glu_in),
        )
        if l < layers - 1:
            fill += (glu_strips,)
        back_last, down_part, fill = plane_scatter(
            *pairs[2:], glu_product, rows_product(hidden, down_grad), fill
        )
        gate_part, up_part = fill[:2]
        if l < layers - 1:
            glu_strips = fill[2]
        sent = [v.reshape(line, u_strip, width) for v in (down_part, gate_part, up_part)]
        sent = jnp.concatenate(sent, 1)
        back, gain_part = zip(
            *[rms_back(v, glu_gain[l], d) for v, d in zip(stream_mid, (back_first, back_last))]
        )
        glu_gain_parts[l] = sum(gain_part)
        grad = [a + b for a, b in zip(grad, back)]
        if l < layers - 1:
            sent, summed = tie_all(sent, summed)
        glu_sum = strip_halves(line_scatter(sent))

        lows = []
        for rows, factor, y in zip(grad, out_factor, raw):
            low = (rows * factor).astype(BF16)
            stat = jnp.mean(low.astype(F32) * y, -1) * (factor * factor)[:, 0]
            lows.append(jnp.concatenate([low, in_parts(stat)], 1))
        out_grad = gathered(lows)
        if l < layers - 1:
            out_grad, summed, glu_strips = tie_all(out_grad, summed, glu_strips)
            glu_strips = strips_far(glu_strips)
            mix_strips = strips_far(strips_near(summed))
        padded = jnp.pad(out_w[l], ((0, 0), (0, LANES)))
        mixed_grad = [matmul_t(rows, padded) for rows in out_grad]
        scanned = mixer.scan_back(mixed_grad, state, out_grad)
        enter = line_carry(scanned[5], scanned[4], True)
        proj_grad, bound_parts[l], out_gain_parts[l] = mixer.project_back(
            mixed_grad, state, out_grad, carry, scanned, enter
        )
        out_part = rows_product(mixed, out_grad)[:, :width]
        mix_part = rows_product(proj_grad, mixer_in)

        def mix_sent(out_part, mix_part):
            mix_part = mix_part.reshape(3, line, c_strip, width).transpose(1, 0, 2, 3)
            mix_part = mix_part.reshape(line, 3 * c_strip, width)
            return jnp.concatenate([mix_part, out_part.reshape(line, c_strip, width)], 1)

        def mix_product(rows):
            return matmul(rows, mix_w[l])

        if l == 0:
            proj_grad, sent = tie_all(proj_grad, mix_sent(out_part, mix_part))
            back_first, glu_sum, _ = plane_scatter(*proj_grad[:2], mix_product, glu_sum)
            back_last, _, (glu_strips, mix_strips) = plane_scatter(
                *proj_grad[2:], mix_product, (), (glu_strips, mix_strips)
            )
            finish_glu(1, glu_strips)
            finish_mix(1, mix_strips)
        else:
            back_first, _, _ = plane_scatter(*proj_grad[:2], mix_product)
            back_last, out_part, mix_part = plane_scatter(
                *proj_grad[2:], mix_product, out_part, mix_part
            )
            sent = mix_sent(out_part, mix_part)
        back, gain_part = zip(
            *[rms_back(v, mix_gain[l], d) for v, d in zip(stream_in, (back_first, back_last))]
        )
        mix_gain_parts[l] = sum(gain_part)
        grad = [a + b for a, b in zip(grad, back)]
        sent, glu_sum = tie_all(sent, glu_sum)
        summed = strip_halves(line_scatter(sent))
    finish_glu(0, strips_far(strips_near(glu_sum)))
    finish_mix(0, strips_far(strips_near(summed)))

    def spread(row):
        zeros = jnp.zeros((line, 2, dp, c_strip), F32)
        return lax.dynamic_update_slice(
            zeros, row.reshape(line, 1, 1, c_strip), (0, core, column, 0)
        ).reshape(-1)

    rows = jnp.stack(
        mix_gain_parts
        + glu_gain_parts
        + [spread(v) for v in out_gain_parts]
        + [spread(v) for v in bound_parts]
    )
    rows = sum_all(rows)
    mix_gain_grad = rows[:layers]
    glu_gain_grad = rows[layers : 2 * layers]
    mine = lax.dynamic_slice_in_dim(rows[2 * layers :], member * channels, channels, 1)
    out_gain_grad = mine[:layers]
    extra = jnp.zeros((bound_vals.shape[0] - layers, channels), F32)
    bound_grad = bound_back(jnp.concatenate([mine[layers:], extra], 0))[0]
    return (
        jnp.concatenate(stream, 0),
        jnp.concatenate(grad, 0),
        grads["mix"],
        grads["mix_out"],
        grads["glu"],
        grads["glu_out"],
        mix_gain_grad,
        out_gain_grad,
        glu_gain_grad,
        bound_grad,
    )


def solution(mesh):
    return jax.shard_map(
        local,
        mesh=mesh,
        in_specs=(
            P(("dp", "mp"), None),
            P(("dp", "mp"), None),
            P("dp"),
            P(None, None, None, "mp"),
            P(None, "mp", None),
            P(None, None, None, "mp"),
            P(None, "mp", None),
            P(),
            P(None, "mp"),
            P(),
            P(None, "mp"),
        ),
        out_specs=(
            P(("dp", "mp"), None),
            P(("dp", "mp"), None),
            P(None, None, None, "mp"),
            P(None, "mp", None),
            P(None, None, None, "mp"),
            P(None, "mp", None),
            P(),
            P(None, "mp"),
            P(),
            P(None, "mp"),
        ),
        check_vma=False,
    )
```

```python
import functools

import jax
import jax.numpy as jnp
from jax import lax
from jax.experimental import pallas as pl
from jax.experimental.pallas import tpu as pltpu
from jax.sharding import PartitionSpec as P

norm_eps = 1e-06
domain_scale = (1.0, 0.5, 2.0)
F32 = jnp.float32
BF16 = jnp.bfloat16
LANES = 128
VMEM_LIMIT = 56 * 1024 * 1024


def high_bit(s):
    return 1 << (s.bit_length() - 1)


def low_bit(s):
    return s & -s


def swap_dp(v, bit):
    return lax.ppermute(v, "dp", [(i, i ^ bit) for i in range(lax.axis_size("dp"))])


def swap_core(v):
    return lax.ppermute(v, "mp", [(i, i ^ 1) for i in range(lax.axis_size("mp"))])


def slot_groups():
    slots = sorted(range(lax.axis_size("dp")), key=lambda s: (bin(s).count("1"), s))
    near = [s for s in slots if bin(s).count("1") <= 1]
    return near, slots[len(near) :]


def join(parts):
    return parts[0] if len(parts) == 1 else jnp.concatenate(parts, 0)


def plane_gather(x):
    near, far = slot_groups()
    half = x.shape[0] // 2
    slots = {0: x}
    for s in near[1:]:
        slots[s] = swap_dp(x, s)
    for s in far:
        top, low = high_bit(s), low_bit(s)
        slots[s] = join([swap_dp(slots[s ^ top][:half], top), swap_dp(slots[s ^ low][half:], low)])
    own = join([slots[s] for s in range(len(slots))])
    return [own, swap_core(own)]


def plane_scatter(own, other, product, first_fill=(), last_fill=()):
    near, far = slot_groups()
    count = own.shape[0] // lax.axis_size("dp")
    half = count // 2
    other = swap_core(product(other).astype(BF16))
    both = product(own) + other.astype(F32)
    total = {s: both[s * count : (s + 1) * count] for s in near + far}
    for s in reversed(far):
        top, low = high_bit(s), low_bit(s)
        first = swap_dp(total[s][:half].astype(BF16), top)
        last = swap_dp(total[s][half:].astype(BF16), low)
        if s == far[0]:
            first, last, first_fill = tie_all(first, last, first_fill)
        total[s ^ top] = join([total[s ^ top][:half] + first.astype(F32), total[s ^ top][half:]])
        total[s ^ low] = join([total[s ^ low][:half], total[s ^ low][half:] + last.astype(F32)])
    got = [swap_dp(total[s].astype(BF16), s) for s in near[1:]]
    got, last_fill = tie_all(got, last_fill)
    out = total[0]
    for v in got:
        out = out + v.astype(F32)
    return out, first_fill, last_fill


def plane_scatter_rows(totals):
    part = totals[:, 0] + swap_core(totals[:, 1])
    while part.shape[0] > 1:
        half = part.shape[0] // 2
        part = part[:half] + swap_dp(part[half:], half)
    return part[0]


def in_parts(vec):
    parts = []
    rest = vec
    for _ in range(3):
        part = lax.reduce_precision(rest, 8, 7)
        rest = rest - part
        parts.append(part.astype(BF16))
    return jnp.pad(jnp.stack(parts, 1), ((0, 0), (0, LANES - 3)))


def strip_halves(v):
    half = v.shape[1] // 32 * 16
    return v[0, :half], v[0, half:]


def strips_near(halves):
    near, _ = slot_groups()
    slots = {0: tuple(halves)}
    for s in near[1:]:
        slots[s] = tuple(swap_dp(v, s) for v in halves)
    return slots


def strips_far(slots):
    near, far = slot_groups()
    slots = dict(slots)
    for s in far:
        top, low = high_bit(s), low_bit(s)
        slots[s] = (swap_dp(slots[s ^ top][0], top), swap_dp(slots[s ^ low][1], low))
    return [slots[s] for s in range(len(slots))]


def in_columns(slots):
    slots = jnp.stack([jnp.concatenate(halves, 0) for halves in slots], 0)
    column = lax.axis_index("dp")
    return jnp.stack(
        [
            lax.dynamic_index_in_dim(slots, column ^ s, 0, keepdims=False)
            for s in range(slots.shape[0])
        ],
        0,
    )


def line_sum(v):
    size = lax.axis_size("mp")
    bit = 2
    while bit < size:
        v = v + lax.ppermute(v, "mp", [(i, i ^ bit) for i in range(size)])
        bit *= 2
    return v


def sum_all(v):
    v = v + swap_core(v)
    bit = 1
    while bit < lax.axis_size("dp"):
        v = v + swap_dp(v, bit)
        bit *= 2
    return line_sum(v)


def tie_all(*values):
    return lax.optimization_barrier(values)


def line_groups():
    size = lax.axis_size("mp")
    return [[place * 2 + core for place in range(size // 2)] for core in (0, 1)]


def line_gather(v):
    return lax.all_gather(v, "mp", axis=0, tiled=False, axis_index_groups=line_groups())


def line_scatter(v):
    return lax.psum_scatter(
        v, "mp", scatter_dimension=0, tiled=True, axis_index_groups=line_groups()
    )


def line_carry(decay, value, ahead):
    size = lax.axis_size("mp")
    packed = jnp.stack([decay, value], 0)
    total = None
    for step in reversed(range(1, size // 2)):
        pairs = [(i, i + 2 * step) for i in range(size - 2 * step)]
        if ahead:
            pairs = [(b, a) for a, b in pairs]
        got = lax.ppermute(packed, "mp", pairs)
        total = got[1] if total is None else got[1] + got[0] * total
    return jnp.zeros_like(value) if total is None else total


def in_order(core, own, other):
    return jnp.where(core == 0, own, other), jnp.where(core == 0, other, own)


def take(refs, count):
    return refs[:count], refs[count:]


class Places:
    def __init__(self, slots, rows):
        self.blocks, self.rows, self.half = 2 * slots, rows, rows // 2

    def __iter__(self):
        for block in range(self.blocks):
            for h in (0, 1):
                here = pl.ds(block * self.rows + h * self.half, self.half)
                part = pl.ds(block // 2 * self.half, self.half)
                yield block, h, here, 2 * h + block % 2, part


def scan_kernel(places, core_ref, *refs):
    pieces, rows = 4, places.rows
    inputs, refs = take(refs, pieces)
    forgets, refs = take(refs, pieces)
    bound_ref, local_ref, decay_ref, end_ref, full_ref, seq_end_ref, seq_full_ref = refs
    blocks = places.blocks
    low = bound_ref[...]
    for _, _, here, p, part in places:
        forget = low + (1.0 - low) * jax.nn.sigmoid(forgets[p][part, :])
        decay_ref[here, :] = forget
        local_ref[here, :] = (1.0 - forget) * jax.nn.silu(inputs[p][part, :])

    def step(t, kept):
        state, decay = kept
        place = pl.ds(t, blocks, stride=rows)
        forget = decay_ref[place, :]
        state = forget * state + local_ref[place, :]
        decay = forget * decay
        local_ref[place, :] = state
        decay_ref[place, :] = decay
        return state, decay

    none = decay_ref[pl.ds(0, blocks, stride=rows), :] * 0.0
    end, full = lax.fori_loop(0, rows, step, (none, none + 1.0), unroll=8)
    end_ref[...] = end
    full_ref[...] = full
    core = core_ref[0]
    own, other = pl.ds(0, blocks // 2, stride=2), pl.ds(1, blocks // 2, stride=2)
    end_a, end_b = in_order(core, end_ref[own, :], end_ref[other, :])
    full_a, full_b = in_order(core, full_ref[own, :], full_ref[other, :])
    seq_end_ref[...] = end_b + full_b * end_a
    seq_full_ref[...] = full_a * full_b


def state_kernel(places, core_ref, *refs):
    pieces = 4
    gates, refs = take(refs, pieces)
    local_ref, decay_ref, end_ref, full_ref, enter_ref, gain_ref = refs[:6]
    state_ref, square_ref, carry_ref = refs[6:9]
    outs = refs[9:]
    core = core_ref[0]
    slots = places.blocks // 2
    own, other = pl.ds(0, slots, stride=2), pl.ds(1, slots, stride=2)
    end_a, _ = in_order(core, end_ref[own, :], end_ref[other, :])
    full_a, _ = in_order(core, full_ref[own, :], full_ref[other, :])
    carry_a = enter_ref[...]
    carry_b = end_a + full_a * carry_a
    carry_own, carry_other = in_order(core, carry_a, carry_b)
    carry_ref[own, :] = carry_own
    carry_ref[other, :] = carry_other
    gain = gain_ref[...]
    for block, h, here, p, part in places:
        row = slice(block, block + 1)
        state = local_ref[here, :] + decay_ref[here, :] * carry_ref[row, :]
        state_ref[here, :] = state
        gated = state * jax.nn.silu(gates[p][part, :])
        outs[p][part, :] = (gated * gain).astype(BF16)
        total = jnp.sum((gated * gated).T, 0, keepdims=True)
        row = slice(h * places.blocks + block, h * places.blocks + block + 1)

        @pl.when(pl.program_id(0) == 0)
        def _(row=row, total=total):
            square_ref[row, :] = total

        @pl.when(pl.program_id(0) > 0)
        def _(row=row, total=total):
            square_ref[row, :] = square_ref[row, :] + total


def row_stat(parts):
    parts = parts.astype(F32)
    return (parts[:, 0:1] + parts[:, 1:2]) + parts[:, 2:3]


def scan_back_kernel(places, core_ref, *refs):
    pieces, rows = 4, places.rows
    grads, refs = take(refs, pieces)
    forgets, refs = take(refs, pieces)
    gates, refs = take(refs, pieces)
    stats, refs = take(refs, pieces)
    state_ref, bound_ref, gain_ref = refs[:3]
    local_ref, decay_ref, end_ref, full_ref, seq_end_ref, seq_full_ref, forget_ref = refs[3:]
    blocks = places.blocks
    low = bound_ref[...]
    gain = gain_ref[...]
    for _, _, here, p, part in places:
        silu_gate = jax.nn.silu(gates[p][part, :])
        gated = state_ref[here, :] * silu_gate
        stat = row_stat(stats[p][part, :])
        local_ref[here, :] = (grads[p][part, :] * gain - gated * stat) * silu_gate
        forget_ref[here, :] = low + (1.0 - low) * jax.nn.sigmoid(forgets[p][part, :])

    def step(k, kept):
        t = rows - 1 - k
        state, decay, forget = kept
        place = pl.ds(t, blocks, stride=rows)
        state = forget * state + local_ref[place, :]
        decay = forget * decay
        local_ref[place, :] = state
        decay_ref[place, :] = decay
        return state, decay, forget_ref[place, :]

    none = forget_ref[pl.ds(0, blocks, stride=rows), :] * 0.0
    state, decay, forget = lax.fori_loop(
        0, rows, step, (none, none + 1.0, none + 1.0), unroll=8
    )
    end_ref[...] = forget * state
    full_ref[...] = forget * decay
    core = core_ref[0]
    own, other = pl.ds(0, blocks // 2, stride=2), pl.ds(1, blocks // 2, stride=2)
    end_a, end_b = in_order(core, end_ref[own, :], end_ref[other, :])
    full_a, full_b = in_order(core, full_ref[own, :], full_ref[other, :])
    seq_end_ref[...] = end_a + full_a * end_b
    seq_full_ref[...] = full_a * full_b


def project_back_kernel(places, core_ref, *refs):
    pieces, half = 4, places.half
    grads, refs = take(refs, pieces)
    inputs, refs = take(refs, pieces)
    forgets, refs = take(refs, pieces)
    gates, refs = take(refs, pieces)
    stats, refs = take(refs, pieces)
    state_ref, bound_ref, gain_ref, carry_ref = refs[:4]
    local_ref, decay_ref, end_ref, full_ref, enter_ref = refs[4:9]
    outs, (bound_grad_ref, gain_grad_ref, back_ref) = take(refs[9:], pieces)
    core = core_ref[0]
    slots = places.blocks // 2
    width = outs[0].shape[1] // 3
    column = pl.program_id(0) * LANES
    own, other = pl.ds(0, slots, stride=2), pl.ds(1, slots, stride=2)
    _, end_b = in_order(core, end_ref[own, :], end_ref[other, :])
    _, full_b = in_order(core, full_ref[own, :], full_ref[other, :])
    carry_b = enter_ref[...]
    carry_a = end_b + full_b * carry_b
    carry_own, carry_other = in_order(core, carry_a, carry_b)
    back_ref[own, :] = carry_own
    back_ref[other, :] = carry_other
    low = bound_ref[...]
    gain = gain_ref[...]
    bound_total = jnp.zeros((1, LANES), F32)
    gain_total = jnp.zeros((1, LANES), F32)
    top = lax.broadcasted_iota(jnp.int32, (half, LANES), 0) == 0
    for block, h, here, p, part in places:
        row = slice(block, block + 1)
        state = state_ref[here, :]
        if h == 0:
            before = carry_ref[row, :]
        else:
            before = state_ref[pl.ds(block * places.rows + half - 1, 1), :]
        before = jnp.where(top, before, pltpu.roll(state, 1, 0))
        gate = gates[p][part, :]
        gate_sig = jax.nn.sigmoid(gate)
        silu_gate = gate * gate_sig
        grad = grads[p][part, :]
        gated = state * silu_gate
        dgated = grad * gain - gated * row_stat(stats[p][part, :])
        dstate = local_ref[here, :] + decay_ref[here, :] * back_ref[row, :]
        enter = inputs[p][part, :]
        enter_sig = jax.nn.sigmoid(enter)
        forget_sig = jax.nn.sigmoid(forgets[p][part, :])
        keep = (1.0 - low) * (1.0 - forget_sig)
        dforget = dstate * (before - enter * enter_sig)
        slope = dforget * (1.0 - forget_sig)
        made = (
            dstate * keep * enter_sig * (1.0 + enter * (1.0 - enter_sig)),
            slope * (1.0 - low) * forget_sig,
            dgated * state * gate_sig * (1.0 + gate * (1.0 - gate_sig)),
        )
        for which, value in enumerate(made):
            lanes = pl.ds(pl.multiple_of(which * width + column, LANES), LANES)
            outs[p][part, lanes] = value.astype(BF16)
        bound_total = bound_total + jnp.sum(slope, 0, keepdims=True)
        gain_total = gain_total + jnp.sum(grad * gated, 0, keepdims=True)
    bound_grad_ref[...] = bound_total
    gain_grad_ref[...] = gain_total


def struct(shape, dtype=F32):
    return jax.ShapeDtypeStruct(shape, dtype)


class Mixer:
    def __init__(self, core, projected, bound, gain):
        self.core, self.projected, self.bound, self.gain = core, projected, bound, gain
        self.total = sum(p.shape[0] for p in projected)
        self.blocks = 2 * lax.axis_size("dp")
        self.rows = self.total // self.blocks
        self.places = Places(lax.axis_size("dp"), self.rows)
        self.channels = projected[0].shape[1] // 3
        self.steps = self.channels // LANES

    def column(self, rows, offset=0):
        return pl.BlockSpec((rows, LANES), lambda i, offset=offset: (0, offset + i))

    def pieces(self, which=0):
        return [self.column(p.shape[0], which * self.steps) for p in self.projected]

    def whole(self, rows, columns):
        return pl.BlockSpec((rows, columns), lambda i: (0, 0))

    def scanned(self):
        sizes = [self.total] * 2 + [self.blocks] * 2 + [self.blocks // 2] * 2
        return [self.column(n) for n in sizes], [struct((n, self.channels)) for n in sizes]

    def call(self, body, name, in_specs, out_specs, out_shapes, scratch, flops, args):
        moved = 1024
        call = pl.pallas_call(
            functools.partial(body, self.places),
            name=name,
            grid=(self.steps,),
            in_specs=[pl.BlockSpec(memory_space=pltpu.SMEM)] + in_specs,
            out_specs=out_specs,
            out_shape=out_shapes,
            scratch_shapes=scratch,
            compiler_params=pltpu.CompilerParams(
                vmem_limit_bytes=VMEM_LIMIT, dimension_semantics=("arbitrary",)
            ),
            cost_estimate=pl.CostEstimate(
                flops=flops, bytes_accessed=moved, transcendentals=0
            ),
        )
        return list(call(self.core, *args))

    def scan(self):
        specs, shapes = self.scanned()
        return self.call(
            scan_kernel,
            "mixer_scan",
            self.pieces(0) + self.pieces(1) + [self.column(1)],
            specs,
            shapes,
            [],
            200,
            self.projected * 2 + [self.bound],
        )

    def state(self, scanned, enter):
        total, blocks, channels = self.total, self.blocks, self.channels
        sizes = [total] * 2 + [blocks] * 2 + [blocks // 2, 1]
        outs = self.call(
            state_kernel,
            "mixer_state",
            self.pieces(2) + [self.column(n) for n in sizes],
            [self.column(total), self.whole(2 * blocks, self.rows // 2), self.column(blocks)]
            + self.pieces(),
            [struct((total, channels)), struct((2 * blocks, self.rows // 2)), struct((blocks, channels))]
            + [struct((p.shape[0], channels), BF16) for p in self.projected],
            [],
            100,
            self.projected + scanned[:4] + [enter, self.gain],
        )
        return outs[0], outs[1], outs[2], list(outs[3:])

    def scan_back(self, grads, state, stats):
        specs, shapes = self.scanned()
        return self.call(
            scan_back_kernel,
            "mixer_scan_back",
            self.pieces()
            + self.pieces(1)
            + self.pieces(2)
            + [
                pl.BlockSpec((p.shape[0], LANES), lambda i, last=p.shape[1] // LANES - 1: (0, last))
                for p in stats
            ]
            + [self.column(self.total)]
            + [self.column(1)] * 2,
            specs,
            shapes,
            [pltpu.VMEM((self.total, LANES), F32)],
            250,
            grads + self.projected * 2 + stats + [state, self.bound, self.gain],
        )

    def project_back(self, grads, state, stats, carry, scanned, enter):
        total, blocks, channels = self.total, self.blocks, self.channels
        sizes = [1, 1, blocks, total, total, blocks, blocks, blocks // 2]
        outs = self.call(
            project_back_kernel,
            "mixer_project_back",
            self.pieces()
            + self.pieces(0)
            + self.pieces(1)
            + self.pieces(2)
            + [
                pl.BlockSpec((p.shape[0], LANES), lambda i, last=p.shape[1] // LANES - 1: (0, last))
                for p in stats
            ]
            + [self.column(total)]
            + [self.column(n) for n in sizes],
            [self.whole(*p.shape) for p in self.projected] + [self.column(1)] * 2,
            [struct(p.shape, BF16) for p in self.projected] + [struct((1, channels))] * 2,
            [pltpu.VMEM((blocks, LANES), F32)],
            200,
            grads
            + self.projected * 3
            + stats
            + [state, self.bound, self.gain, carry]
            + scanned[:4]
            + [enter],
        )
        return list(outs[:-2]), outs[-2], outs[-1]


def strip_rows(first, last, start, size):
    split = first.shape[0]
    found = []
    if start < split:
        count = min(start + size, split) - start
        found.append((0, first[pl.ds(start, count), :]))
    if start + size > split:
        begin = max(start, split)
        found.append((begin - start, last[pl.ds(begin - split, start + size - begin), :]))
    return found


def place_glu_kernel(count, column_ref, *refs):
    out_ref, glu_ref = refs[-2:]
    size = out_ref.shape[1] // count
    for s in range(count):
        at = (column_ref[0] ^ s) * size
        for which in range(3):
            for offset, rows in strip_rows(refs[2 * s], refs[2 * s + 1], which * size, size):
                here = pl.ds(pl.multiple_of(at + offset, 16), rows.shape[0])
                if which == 0:
                    out_ref[0, here, :] = rows.astype(F32)
                else:
                    glu_ref[0, which - 1, here, :] = rows.astype(F32)


def place_mix_kernel(count, column_ref, *refs):
    out_ref, mix_ref, turn_ref = refs[-3:]
    size = out_ref.shape[1] // count
    for which in range(4):
        for s in range(count):
            at = (column_ref[0] ^ s) * size
            for offset, rows in strip_rows(refs[2 * s], refs[2 * s + 1], which * size, size):
                here = pl.ds(pl.multiple_of(at + offset, 16), rows.shape[0])
                if which == 3:
                    out_ref[0, here, :] = rows.astype(F32)
                else:
                    turn_ref[here, :] = rows.astype(F32)
        if which < 3:
            mix_ref[0, which] = turn_ref[...].T


def place_strips(body, name, layer, column, slots, kept, shapes, blocks, indices, scratch):
    flat = [v for halves in slots for v in halves]
    lanes = blocks[0][-1]
    kept = list(kept or ())
    return pl.pallas_call(
        functools.partial(body, len(slots)),
        name=name,
        grid=(flat[0].shape[1] // lanes,),
        in_specs=[pl.BlockSpec(memory_space=pltpu.SMEM)]
        + [pl.BlockSpec((v.shape[0], lanes), lambda i: (0, i)) for v in flat]
        + [pl.BlockSpec(memory_space=pl.ANY) for _ in kept],
        out_specs=[
            pl.BlockSpec(block, lambda i, index=index: (layer,) + index(i))
            for block, index in zip(blocks, indices)
        ],
        out_shape=[jax.ShapeDtypeStruct(shape, F32) for shape in shapes],
        scratch_shapes=scratch,
        input_output_aliases={1 + len(flat) + k: k for k in range(len(kept))},
        compiler_params=pltpu.CompilerParams(
            vmem_limit_bytes=VMEM_LIMIT, dimension_semantics=("arbitrary",)
        ),
        cost_estimate=pl.CostEstimate(flops=100, bytes_accessed=1024, transcendentals=0),
    )(column, *flat, *kept)


def matmul(a, b):
    return jnp.dot(a, b, preferred_element_type=F32)


def matmul_t(a, b):
    return lax.dot_general(a, b, (((1,), (1,)), ((), ())), preferred_element_type=F32)


def matmul_rows(a, b):
    return lax.dot_general(a, b, (((0,), (0,)), ((), ())), preferred_element_type=F32)


def rows_product(a, b):
    return matmul_rows(join(a), join(b)).astype(BF16)


@jax.tree_util.register_pytree_node_class
class Pair:
    def __init__(self, a, b):
        self.a, self.b = a, b

    @property
    def shape(self):
        return self.a.shape

    def __getitem__(self, part):
        return Pair(self.a[part], self.b[part])

    def tree_flatten(self):
        return (self.a, self.b), None

    @classmethod
    def tree_unflatten(cls, _, parts):
        return cls(*parts)


def rms_factor(values):
    return lax.rsqrt(jnp.mean(values * values, -1, keepdims=True) + norm_eps)


def rms_back(values, gain, grad):
    factor = rms_factor(values)
    normed = values * factor
    scaled = grad * gain
    back = factor * (scaled - normed * jnp.mean(scaled * normed, -1, keepdims=True))
    return back, jnp.sum(grad * normed, 0)


def bound_rows(logits):
    return jnp.cumsum(jax.nn.softmax(logits, 0), 0)


def local(
    hidden_in,
    cotangent,
    domain_tags,
    mix_weight,
    mix_out_weight,
    glu_weight,
    glu_out_weight,
    mix_gain,
    out_gain,
    glu_gain,
    bound_logits,
):
    dp = lax.axis_size("dp")
    line = lax.axis_size("mp") // 2
    column = lax.axis_index("dp")
    member = lax.axis_index("mp")
    core = member % 2
    core_arg = core.astype(jnp.int32).reshape(1)
    width = hidden_in.shape[1]
    layers = mix_weight.shape[0]
    channels = mix_weight.shape[3]
    units = glu_weight.shape[3]
    c_strip, u_strip = channels // dp, units // dp

    def cut(array, axis, size):
        return lax.dynamic_slice_in_dim(array, column * size, size, axis)

    scale_table = jnp.array(domain_scale, dtype=F32)
    match = domain_tags[0] == jnp.arange(3, dtype=jnp.int32)
    grad = cotangent.astype(F32) * jnp.sum(jnp.where(match, scale_table, 0.0))
    bound_vals, bound_back = jax.vjp(bound_rows, bound_logits)

    mix_w, out_w, gate_w, up_w, down_w = ([None] * layers for _ in range(5))

    def mix_strip(weight, out=None):
        strip = cut(weight, 2, c_strip).transpose(1, 2, 0).reshape(3 * c_strip, width)
        return strip if out is None else jnp.concatenate([strip, cut(out, 0, c_strip)], 0)

    def glu_strip(weight):
        return cut(weight, 2, u_strip).transpose(1, 2, 0).reshape(2 * u_strip, width)

    def gather_mix(l, strip, out=None):
        got = line_gather(strip)
        mixes = got[:, : 3 * c_strip].reshape(line, 3, c_strip, width).transpose(1, 0, 2, 3)
        mix_w[l] = mixes.reshape(3 * line * c_strip, width)
        out = got[:, 3 * c_strip :] if out is None else line_gather(out)
        out_w[l] = out.reshape(line * c_strip, width)

    def gather_glu(l, strip):
        got = line_gather(strip)
        gate_w[l] = got[:, :u_strip].reshape(line * u_strip, width)
        up_w[l] = got[:, u_strip:].reshape(line * u_strip, width)

    def gather_down(l, strip):
        down_w[l] = line_gather(strip).reshape(line * u_strip, width)

    strip = mix_strip(mix_weight[0])
    strip, hidden_in, out_strip = tie_all(strip, hidden_in, mix_out_weight[0])
    gather_mix(0, strip, cut(out_strip, 0, c_strip))
    half = hidden_in.shape[0] // 2

    def halves(rows):
        return [rows[:half], rows[half:]]

    def gathered(lows):
        return [piece for low in lows for piece in plane_gather(low)]

    def normed(rows, gain):
        return (rows * rms_factor(rows) * gain).astype(BF16)

    grad = halves(grad)
    stream = halves(hidden_in.astype(F32))
    kept = []
    for l in range(layers):
        stream_in = stream
        lows = [normed(rows, mix_gain[l]) for rows in stream]
        if l == 0:
            small = jnp.concatenate([cut(bound_vals, 1, c_strip), cut(out_gain, 1, c_strip)], 0)
            lows, small, first_glu = tie_all(lows, small, glu_weight[0])
            strip, down = tie_all(glu_strip(first_glu), glu_out_weight[0])
            gather_glu(0, strip)
            down_strip = cut(down, 0, u_strip)
            small = lax.dynamic_update_slice(
                jnp.zeros((small.shape[0], line, c_strip), F32), small[:, None], (0, member // 2, 0)
            )
            small = line_sum(small).reshape(-1, line * c_strip)
            bounds = [small[i : i + 1] for i in range(layers)]
            gains = [small[bound_vals.shape[0] + i :][:1] for i in range(layers)]
        mixer_in = gathered(lows)
        projected = [matmul_t(rows, mix_w[l]) for rows in mixer_in]
        mixer = Mixer(core_arg, projected, bounds[l], gains[l])
        scanned = mixer.scan()
        enter = line_carry(scanned[5], scanned[4], False)
        state, squares, carry, mixed = mixer.state(scanned, enter)
        if l + 1 < layers:
            down_strip, *raws = tie_all(
                down_strip, mix_weight[l + 1], mix_out_weight[l + 1], glu_weight[l + 1]
            )
            gather_down(l, down_strip)
            strip, raw = tie_all(mix_strip(*raws[:2]), raws[2])
            gather_mix(l + 1, strip)
            strip, down = tie_all(glu_strip(raw), glu_out_weight[l + 1])
            gather_glu(l + 1, strip)
            down_strip = cut(down, 0, u_strip)
        else:
            gather_down(l, down_strip)
        squares = plane_scatter_rows(
            squares.reshape(2, dp, 2, half).transpose(1, 2, 0, 3).reshape(dp, 2, 2 * half)
        )
        out_factor = halves(lax.rsqrt(squares / width + norm_eps)[:, None])
        raw = [
            plane_scatter(*mixed[2 * h : 2 * h + 2], lambda rows, w=out_w[l]: matmul(rows, w))[0]
            for h in (0, 1)
        ]
        stream_mid = [a + b * c for a, b, c in zip(stream, raw, out_factor)]
        glu_in = gathered([normed(rows, glu_gain[l]) for rows in stream_mid])

        def glu(rows):
            a, b = matmul_t(rows, gate_w[l]), matmul_t(rows, up_w[l])
            return a, b, (jax.nn.silu(a) * b).astype(BF16)

        if l == 0:
            glu_in, grad_low = tie_all(glu_in, [rows.astype(BF16) for rows in grad])
            last_grad = gathered(grad_low)
        gate, up, hidden = zip(*[glu(rows) for rows in glu_in])
        if l == 0:
            hidden, last_grad = tie_all(hidden, last_grad)
        stream = [
            stream_mid[h]
            + plane_scatter(*hidden[2 * h : 2 * h + 2], lambda rows, w=down_w[l]: matmul(rows, w))[0]
            for h in (0, 1)
        ]
        kept.append(
            (
                stream_in,
                mixer_in,
                mixer,
                state,
                carry,
                mixed,
                out_factor,
                raw,
                stream_mid,
                glu_in,
                gate,
                up,
                hidden,
            )
        )

    mix_gain_parts = [None] * layers
    glu_gain_parts = [None] * layers
    out_gain_parts = [None] * layers
    bound_parts = [None] * layers

    grads = {}

    def place(name, l, value):
        if name not in grads:
            grads[name] = jnp.zeros((layers,) + value.shape, F32)
        grads[name] = lax.dynamic_update_index_in_dim(grads[name], value.astype(F32), l, 0)

    column_arg = column.astype(jnp.int32).reshape(1)
    lanes = 512
    aligned = u_strip % 16 == 0 and width % lanes == 0

    def finish_glu(l, slots):
        if aligned:
            grads["glus"] = place_strips(
                place_glu_kernel,
                "place_glu",
                l,
                column_arg,
                slots,
                grads.get("glus"),
                [(layers, units, width), (layers, 2, units, width)],
                [(1, units, lanes), (1, 2, units, lanes)],
                [lambda i: (0, i), lambda i: (0, 0, i)],
                [],
            )
            grads["glu_out"] = grads["glus"][0]
            grads["glu"] = grads["glus"][1].transpose(0, 3, 1, 2)
            return
        strips = in_columns(slots)
        place("glu_out", l, strips[:, :u_strip].reshape(units, width))
        strips = strips[:, u_strip:].reshape(dp, 2, u_strip, width).transpose(3, 1, 0, 2)
        place("glu", l, strips.reshape(width, 2, units))

    def finish_mix(l, slots):
        grads["mixes"] = place_strips(
            place_mix_kernel,
            "place_mix",
            l,
            column_arg,
            slots,
            grads.get("mixes"),
            [(layers, channels, width), (layers, 3, width, channels)],
            [(1, channels, lanes), (1, 3, lanes, channels)],
            [lambda i: (0, i), lambda i: (0, i, 0)],
            [pltpu.VMEM((channels, lanes), F32)],
        )
        grads["mix_out"] = grads["mixes"][0]
        grads["mix"] = grads["mixes"][1].transpose(0, 2, 1, 3)

    for l in reversed(range(layers)):
        (
            stream_in,
            mixer_in,
            mixer,
            state,
            carry,
            mixed,
            out_factor,
            raw,
            stream_mid,
            glu_in,
            gate,
            up,
            hidden,
        ) = kept[l]
        if l == layers - 1:
            down_grad = last_grad
        else:
            down_grad = gathered([rows.astype(BF16) for rows in grad])
            down_grad, glu_sum = tie_all(down_grad, glu_sum)
            glu_strips = strips_near(glu_sum)

        def glu_back(rows, a, b):
            dhidden = matmul_t(rows, down_w[l])
            sig = jax.nn.sigmoid(a)
            dgate = (dhidden * b * sig * (1.0 + a * (1.0 - sig))).astype(BF16)
            return Pair(dgate, (dhidden * a * sig).astype(BF16))

        def glu_product(rows):
            return matmul(rows.a, gate_w[l]) + matmul(rows.b, up_w[l])

        pairs = [glu_back(*args) for args in zip(down_grad, gate, up)]
        back_first, _, _ = plane_scatter(*pairs[:2], glu_product)
        fill = (
            rows_product([p.a for p in pairs], glu_in),
            rows_product([p.b for p in pairs], glu_in),
        )
        if l < layers - 1:
            fill += (glu_strips,)
        back_last, down_part, fill = plane_scatter(
            *pairs[2:], glu_product, rows_product(hidden, down_grad), fill
        )
        gate_part, up_part = fill[:2]
        if l < layers - 1:
            glu_strips = fill[2]
        sent = [v.reshape(line, u_strip, width) for v in (down_part, gate_part, up_part)]
        sent = jnp.concatenate(sent, 1)
        back, gain_part = zip(
            *[rms_back(v, glu_gain[l], d) for v, d in zip(stream_mid, (back_first, back_last))]
        )
        glu_gain_parts[l] = sum(gain_part)
        grad = [a + b for a, b in zip(grad, back)]
        if l < layers - 1:
            sent, summed = tie_all(sent, summed)
        glu_sum = strip_halves(line_scatter(sent))

        lows = []
        for rows, factor, y in zip(grad, out_factor, raw):
            low = (rows * factor).astype(BF16)
            stat = jnp.mean(low.astype(F32) * y, -1) * (factor * factor)[:, 0]
            lows.append(jnp.concatenate([low, in_parts(stat)], 1))
        out_grad = gathered(lows)
        if l < layers - 1:
            glu_strips = strips_far(glu_strips)
            mix_strips = strips_far(strips_near(summed))
        padded = jnp.pad(out_w[l], ((0, 0), (0, LANES)))
        mixed_grad = [matmul_t(rows, padded) for rows in out_grad]
        scanned = mixer.scan_back(mixed_grad, state, out_grad)
        enter = line_carry(scanned[5], scanned[4], True)
        proj_grad, bound_parts[l], out_gain_parts[l] = mixer.project_back(
            mixed_grad, state, out_grad, carry, scanned, enter
        )
        out_part = rows_product(mixed, out_grad)[:, :width]
        mix_part = rows_product(proj_grad, mixer_in)

        def mix_sent(out_part, mix_part):
            mix_part = mix_part.reshape(3, line, c_strip, width).transpose(1, 0, 2, 3)
            mix_part = mix_part.reshape(line, 3 * c_strip, width)
            return jnp.concatenate([mix_part, out_part.reshape(line, c_strip, width)], 1)

        def mix_product(rows):
            return matmul(rows, mix_w[l])

        if l == 0:
            sent = mix_sent(out_part, mix_part)
            proj_grad, sent, glu_sum, glu_strips, mix_strips = tie_all(
                proj_grad, sent, glu_sum, glu_strips, mix_strips
            )
            back_first, _, _ = plane_scatter(*proj_grad[:2], mix_product)
            back_last, _, _ = plane_scatter(*proj_grad[2:], mix_product)
            finish_glu(1, glu_strips)
            finish_mix(1, mix_strips)
        else:
            back_first, _, _ = plane_scatter(*proj_grad[:2], mix_product)
            back_last, out_part, mix_part = plane_scatter(
                *proj_grad[2:], mix_product, out_part, mix_part
            )
            sent = mix_sent(out_part, mix_part)
        back, gain_part = zip(
            *[rms_back(v, mix_gain[l], d) for v, d in zip(stream_in, (back_first, back_last))]
        )
        mix_gain_parts[l] = sum(gain_part)
        grad = [a + b for a, b in zip(grad, back)]
        if l > 0:
            sent, glu_sum = tie_all(sent, glu_sum)
        summed = strip_halves(line_scatter(sent))
        if l == 0:
            grad, summed = tie_all(grad, summed)
    finish_glu(0, strips_far(strips_near(glu_sum)))
    finish_mix(0, strips_far(strips_near(summed)))

    def spread(row):
        zeros = jnp.zeros((line, 2, dp, c_strip), F32)
        return lax.dynamic_update_slice(
            zeros, row.reshape(line, 1, 1, c_strip), (0, core, column, 0)
        ).reshape(-1)

    rows = jnp.stack(
        mix_gain_parts
        + glu_gain_parts
        + [spread(v) for v in out_gain_parts]
        + [spread(v) for v in bound_parts]
    )
    rows = sum_all(rows)
    mix_gain_grad = rows[:layers]
    glu_gain_grad = rows[layers : 2 * layers]
    mine = lax.dynamic_slice_in_dim(rows[2 * layers :], member * channels, channels, 1)
    out_gain_grad = mine[:layers]
    extra = jnp.zeros((bound_vals.shape[0] - layers, channels), F32)
    bound_grad = bound_back(jnp.concatenate([mine[layers:], extra], 0))[0]
    return (
        jnp.concatenate(stream, 0),
        jnp.concatenate(grad, 0),
        grads["mix"],
        grads["mix_out"],
        grads["glu"],
        grads["glu_out"],
        mix_gain_grad,
        out_gain_grad,
        glu_gain_grad,
        bound_grad,
    )


def solution(mesh):
    return jax.shard_map(
        local,
        mesh=mesh,
        in_specs=(
            P(("dp", "mp"), None),
            P(("dp", "mp"), None),
            P("dp"),
            P(None, None, None, "mp"),
            P(None, "mp", None),
            P(None, None, None, "mp"),
            P(None, "mp", None),
            P(),
            P(None, "mp"),
            P(),
            P(None, "mp"),
        ),
        out_specs=(
            P(("dp", "mp"), None),
            P(("dp", "mp"), None),
            P(None, None, None, "mp"),
            P(None, "mp", None),
            P(None, None, None, "mp"),
            P(None, "mp", None),
            P(),
            P(None, "mp"),
            P(),
            P(None, "mp"),
        ),
        check_vma=False,
    )
```

```python
import functools

import jax
import jax.numpy as jnp
from jax import lax
from jax.experimental import pallas as pl
from jax.experimental.pallas import tpu as pltpu
from jax.sharding import PartitionSpec as P

norm_eps = 1e-06
domain_scale = (1.0, 0.5, 2.0)
F32 = jnp.float32
BF16 = jnp.bfloat16
LANES = 128
VMEM_LIMIT = 56 * 1024 * 1024


def high_bit(s):
    return 1 << (s.bit_length() - 1)


def low_bit(s):
    return s & -s


def swap_dp(v, bit):
    return lax.ppermute(v, "dp", [(i, i ^ bit) for i in range(lax.axis_size("dp"))])


def swap_core(v):
    return lax.ppermute(v, "mp", [(i, i ^ 1) for i in range(lax.axis_size("mp"))])


def slot_groups():
    slots = sorted(range(lax.axis_size("dp")), key=lambda s: (bin(s).count("1"), s))
    near = [s for s in slots if bin(s).count("1") <= 1]
    return near, slots[len(near) :]


def join(parts):
    return parts[0] if len(parts) == 1 else jnp.concatenate(parts, 0)


def plane_gather(x):
    near, far = slot_groups()
    half = x.shape[0] // 2
    slots = {0: x}
    for s in near[1:]:
        slots[s] = swap_dp(x, s)
    for s in far:
        top, low = high_bit(s), low_bit(s)
        slots[s] = join([swap_dp(slots[s ^ top][:half], top), swap_dp(slots[s ^ low][half:], low)])
    own = join([slots[s] for s in range(len(slots))])
    return [own, swap_core(own)]


def plane_scatter(own, other, product, first_fill=(), last_fill=()):
    near, far = slot_groups()
    count = own.shape[0] // lax.axis_size("dp")
    half = count // 2
    other = swap_core(product(other).astype(BF16))
    both = product(own) + other.astype(F32)
    total = {s: both[s * count : (s + 1) * count] for s in near + far}
    for s in reversed(far):
        top, low = high_bit(s), low_bit(s)
        first = swap_dp(total[s][:half].astype(BF16), top)
        last = swap_dp(total[s][half:].astype(BF16), low)
        if s == far[0]:
            first, last, first_fill = tie_all(first, last, first_fill)
        total[s ^ top] = join([total[s ^ top][:half] + first.astype(F32), total[s ^ top][half:]])
        total[s ^ low] = join([total[s ^ low][:half], total[s ^ low][half:] + last.astype(F32)])
    got = [swap_dp(total[s].astype(BF16), s) for s in near[1:]]
    got, last_fill = tie_all(got, last_fill)
    out = total[0]
    for v in got:
        out = out + v.astype(F32)
    return out, first_fill, last_fill


def plane_scatter_rows(totals):
    part = totals[:, 0] + swap_core(totals[:, 1])
    while part.shape[0] > 1:
        half = part.shape[0] // 2
        part = part[:half] + swap_dp(part[half:], half)
    return part[0]


def in_parts(vec):
    parts = []
    rest = vec
    for _ in range(3):
        part = lax.reduce_precision(rest, 8, 7)
        rest = rest - part
        parts.append(part.astype(BF16))
    return jnp.pad(jnp.stack(parts, 1), ((0, 0), (0, LANES - 3)))


def strip_halves(v):
    half = v.shape[1] // 32 * 16
    return v[0, :half], v[0, half:]


def strips_near(halves):
    near, _ = slot_groups()
    slots = {0: tuple(halves)}
    for s in near[1:]:
        slots[s] = tuple(swap_dp(v, s) for v in halves)
    return slots


def strips_far(slots):
    near, far = slot_groups()
    slots = dict(slots)
    for s in far:
        top, low = high_bit(s), low_bit(s)
        slots[s] = (swap_dp(slots[s ^ top][0], top), swap_dp(slots[s ^ low][1], low))
    return [slots[s] for s in range(len(slots))]


def in_columns(slots):
    slots = jnp.stack([jnp.concatenate(halves, 0) for halves in slots], 0)
    column = lax.axis_index("dp")
    return jnp.stack(
        [
            lax.dynamic_index_in_dim(slots, column ^ s, 0, keepdims=False)
            for s in range(slots.shape[0])
        ],
        0,
    )


def line_sum(v):
    size = lax.axis_size("mp")
    bit = 2
    while bit < size:
        v = v + lax.ppermute(v, "mp", [(i, i ^ bit) for i in range(size)])
        bit *= 2
    return v


def sum_all(v):
    v = line_sum(v)
    v = v + swap_core(v)
    bit = 1
    while bit < lax.axis_size("dp"):
        v = v + swap_dp(v, bit)
        bit *= 2
    return v


def tie_all(*values):
    return lax.optimization_barrier(values)


def line_groups():
    size = lax.axis_size("mp")
    return [[place * 2 + core for place in range(size // 2)] for core in (0, 1)]


def line_gather(v):
    return lax.all_gather(v, "mp", axis=0, tiled=False, axis_index_groups=line_groups())


def line_scatter(v):
    return lax.psum_scatter(
        v, "mp", scatter_dimension=0, tiled=True, axis_index_groups=line_groups()
    )


def line_carry(decay, value, ahead):
    size = lax.axis_size("mp")
    packed = jnp.stack([decay, value], 0)
    total = None
    for step in reversed(range(1, size // 2)):
        pairs = [(i, i + 2 * step) for i in range(size - 2 * step)]
        if ahead:
            pairs = [(b, a) for a, b in pairs]
        got = lax.ppermute(packed, "mp", pairs)
        total = got[1] if total is None else got[1] + got[0] * total
    return jnp.zeros_like(value) if total is None else total


def in_order(core, own, other):
    return jnp.where(core == 0, own, other), jnp.where(core == 0, other, own)


def take(refs, count):
    return refs[:count], refs[count:]


class Places:
    def __init__(self, slots, rows):
        self.blocks, self.rows, self.half = 2 * slots, rows, rows // 2

    def __iter__(self):
        for block in range(self.blocks):
            for h in (0, 1):
                here = pl.ds(block * self.rows + h * self.half, self.half)
                part = pl.ds(block // 2 * self.half, self.half)
                yield block, h, here, 2 * h + block % 2, part


def scan_kernel(places, core_ref, *refs):
    pieces, rows = 4, places.rows
    inputs, refs = take(refs, pieces)
    forgets, refs = take(refs, pieces)
    bound_ref, local_ref, decay_ref, end_ref, full_ref, seq_end_ref, seq_full_ref = refs
    blocks = places.blocks
    low = bound_ref[...]
    for _, _, here, p, part in places:
        forget = low + (1.0 - low) * jax.nn.sigmoid(forgets[p][part, :])
        decay_ref[here, :] = forget
        local_ref[here, :] = (1.0 - forget) * jax.nn.silu(inputs[p][part, :])

    def step(t, kept):
        state, decay = kept
        place = pl.ds(t, blocks, stride=rows)
        forget = decay_ref[place, :]
        state = forget * state + local_ref[place, :]
        decay = forget * decay
        local_ref[place, :] = state
        decay_ref[place, :] = decay
        return state, decay

    none = decay_ref[pl.ds(0, blocks, stride=rows), :] * 0.0
    end, full = lax.fori_loop(0, rows, step, (none, none + 1.0), unroll=8)
    end_ref[...] = end
    full_ref[...] = full
    core = core_ref[0]
    own, other = pl.ds(0, blocks // 2, stride=2), pl.ds(1, blocks // 2, stride=2)
    end_a, end_b = in_order(core, end_ref[own, :], end_ref[other, :])
    full_a, full_b = in_order(core, full_ref[own, :], full_ref[other, :])
    seq_end_ref[...] = end_b + full_b * end_a
    seq_full_ref[...] = full_a * full_b


def state_kernel(places, core_ref, *refs):
    pieces = 4
    gates, refs = take(refs, pieces)
    local_ref, decay_ref, end_ref, full_ref, enter_ref, gain_ref = refs[:6]
    state_ref, square_ref, carry_ref = refs[6:9]
    outs = refs[9:]
    core = core_ref[0]
    slots = places.blocks // 2
    own, other = pl.ds(0, slots, stride=2), pl.ds(1, slots, stride=2)
    end_a, _ = in_order(core, end_ref[own, :], end_ref[other, :])
    full_a, _ = in_order(core, full_ref[own, :], full_ref[other, :])
    carry_a = enter_ref[...]
    carry_b = end_a + full_a * carry_a
    carry_own, carry_other = in_order(core, carry_a, carry_b)
    carry_ref[own, :] = carry_own
    carry_ref[other, :] = carry_other
    gain = gain_ref[...]
    for block, h, here, p, part in places:
        row = slice(block, block + 1)
        state = local_ref[here, :] + decay_ref[here, :] * carry_ref[row, :]
        state_ref[here, :] = state
        gated = state * jax.nn.silu(gates[p][part, :])
        outs[p][part, :] = (gated * gain).astype(BF16)
        total = jnp.sum((gated * gated).T, 0, keepdims=True)
        row = slice(h * places.blocks + block, h * places.blocks + block + 1)

        @pl.when(pl.program_id(0) == 0)
        def _(row=row, total=total):
            square_ref[row, :] = total

        @pl.when(pl.program_id(0) > 0)
        def _(row=row, total=total):
            square_ref[row, :] = square_ref[row, :] + total


def row_stat(parts):
    parts = parts.astype(F32)
    return (parts[:, 0:1] + parts[:, 1:2]) + parts[:, 2:3]


def scan_back_kernel(places, core_ref, *refs):
    pieces, rows = 4, places.rows
    grads, refs = take(refs, pieces)
    forgets, refs = take(refs, pieces)
    gates, refs = take(refs, pieces)
    stats, refs = take(refs, pieces)
    state_ref, bound_ref, gain_ref = refs[:3]
    local_ref, decay_ref, end_ref, full_ref, seq_end_ref, seq_full_ref, forget_ref = refs[3:]
    blocks = places.blocks
    low = bound_ref[...]
    gain = gain_ref[...]
    for _, _, here, p, part in places:
        silu_gate = jax.nn.silu(gates[p][part, :])
        gated = state_ref[here, :] * silu_gate
        stat = row_stat(stats[p][part, :])
        local_ref[here, :] = (grads[p][part, :] * gain - gated * stat) * silu_gate
        forget_ref[here, :] = low + (1.0 - low) * jax.nn.sigmoid(forgets[p][part, :])

    def step(k, kept):
        t = rows - 1 - k
        state, decay, forget = kept
        place = pl.ds(t, blocks, stride=rows)
        state = forget * state + local_ref[place, :]
        decay = forget * decay
        local_ref[place, :] = state
        decay_ref[place, :] = decay
        return state, decay, forget_ref[place, :]

    none = forget_ref[pl.ds(0, blocks, stride=rows), :] * 0.0
    state, decay, forget = lax.fori_loop(
        0, rows, step, (none, none + 1.0, none + 1.0), unroll=8
    )
    end_ref[...] = forget * state
    full_ref[...] = forget * decay
    core = core_ref[0]
    own, other = pl.ds(0, blocks // 2, stride=2), pl.ds(1, blocks // 2, stride=2)
    end_a, end_b = in_order(core, end_ref[own, :], end_ref[other, :])
    full_a, full_b = in_order(core, full_ref[own, :], full_ref[other, :])
    seq_end_ref[...] = end_a + full_a * end_b
    seq_full_ref[...] = full_a * full_b


def project_back_kernel(places, core_ref, *refs):
    pieces, half = 4, places.half
    grads, refs = take(refs, pieces)
    inputs, refs = take(refs, pieces)
    forgets, refs = take(refs, pieces)
    gates, refs = take(refs, pieces)
    stats, refs = take(refs, pieces)
    state_ref, bound_ref, gain_ref, carry_ref = refs[:4]
    local_ref, decay_ref, end_ref, full_ref, enter_ref = refs[4:9]
    outs, (bound_grad_ref, gain_grad_ref, back_ref) = take(refs[9:], pieces)
    core = core_ref[0]
    slots = places.blocks // 2
    width = outs[0].shape[1] // 3
    column = pl.program_id(0) * LANES
    own, other = pl.ds(0, slots, stride=2), pl.ds(1, slots, stride=2)
    _, end_b = in_order(core, end_ref[own, :], end_ref[other, :])
    _, full_b = in_order(core, full_ref[own, :], full_ref[other, :])
    carry_b = enter_ref[...]
    carry_a = end_b + full_b * carry_b
    carry_own, carry_other = in_order(core, carry_a, carry_b)
    back_ref[own, :] = carry_own
    back_ref[other, :] = carry_other
    low = bound_ref[...]
    gain = gain_ref[...]
    bound_total = jnp.zeros((1, LANES), F32)
    gain_total = jnp.zeros((1, LANES), F32)
    top = lax.broadcasted_iota(jnp.int32, (half, LANES), 0) == 0
    for block, h, here, p, part in places:
        row = slice(block, block + 1)
        state = state_ref[here, :]
        if h == 0:
            before = carry_ref[row, :]
        else:
            before = state_ref[pl.ds(block * places.rows + half - 1, 1), :]
        before = jnp.where(top, before, pltpu.roll(state, 1, 0))
        gate = gates[p][part, :]
        gate_sig = jax.nn.sigmoid(gate)
        silu_gate = gate * gate_sig
        grad = grads[p][part, :]
        gated = state * silu_gate
        dgated = grad * gain - gated * row_stat(stats[p][part, :])
        dstate = local_ref[here, :] + decay_ref[here, :] * back_ref[row, :]
        enter = inputs[p][part, :]
        enter_sig = jax.nn.sigmoid(enter)
        forget_sig = jax.nn.sigmoid(forgets[p][part, :])
        keep = (1.0 - low) * (1.0 - forget_sig)
        dforget = dstate * (before - enter * enter_sig)
        slope = dforget * (1.0 - forget_sig)
        made = (
            dstate * keep * enter_sig * (1.0 + enter * (1.0 - enter_sig)),
            slope * (1.0 - low) * forget_sig,
            dgated * state * gate_sig * (1.0 + gate * (1.0 - gate_sig)),
        )
        for which, value in enumerate(made):
            lanes = pl.ds(pl.multiple_of(which * width + column, LANES), LANES)
            outs[p][part, lanes] = value.astype(BF16)
        bound_total = bound_total + jnp.sum(slope, 0, keepdims=True)
        gain_total = gain_total + jnp.sum(grad * gated, 0, keepdims=True)
    bound_grad_ref[...] = bound_total
    gain_grad_ref[...] = gain_total


def struct(shape, dtype=F32):
    return jax.ShapeDtypeStruct(shape, dtype)


class Mixer:
    def __init__(self, core, projected, bound, gain):
        self.core, self.projected, self.bound, self.gain = core, projected, bound, gain
        self.total = sum(p.shape[0] for p in projected)
        self.blocks = 2 * lax.axis_size("dp")
        self.rows = self.total // self.blocks
        self.places = Places(lax.axis_size("dp"), self.rows)
        self.channels = projected[0].shape[1] // 3
        self.steps = self.channels // LANES

    def column(self, rows, offset=0):
        return pl.BlockSpec((rows, LANES), lambda i, offset=offset: (0, offset + i))

    def pieces(self, which=0):
        return [self.column(p.shape[0], which * self.steps) for p in self.projected]

    def whole(self, rows, columns):
        return pl.BlockSpec((rows, columns), lambda i: (0, 0))

    def scanned(self):
        sizes = [self.total] * 2 + [self.blocks] * 2 + [self.blocks // 2] * 2
        return [self.column(n) for n in sizes], [struct((n, self.channels)) for n in sizes]

    def call(self, body, name, in_specs, out_specs, out_shapes, scratch, flops, args):
        moved = 1024
        call = pl.pallas_call(
            functools.partial(body, self.places),
            name=name,
            grid=(self.steps,),
            in_specs=[pl.BlockSpec(memory_space=pltpu.SMEM)] + in_specs,
            out_specs=out_specs,
            out_shape=out_shapes,
            scratch_shapes=scratch,
            compiler_params=pltpu.CompilerParams(
                vmem_limit_bytes=VMEM_LIMIT, dimension_semantics=("arbitrary",)
            ),
            cost_estimate=pl.CostEstimate(
                flops=flops, bytes_accessed=moved, transcendentals=0
            ),
        )
        return list(call(self.core, *args))

    def scan(self):
        specs, shapes = self.scanned()
        return self.call(
            scan_kernel,
            "mixer_scan",
            self.pieces(0) + self.pieces(1) + [self.column(1)],
            specs,
            shapes,
            [],
            200,
            self.projected * 2 + [self.bound],
        )

    def state(self, scanned, enter):
        total, blocks, channels = self.total, self.blocks, self.channels
        sizes = [total] * 2 + [blocks] * 2 + [blocks // 2, 1]
        outs = self.call(
            state_kernel,
            "mixer_state",
            self.pieces(2) + [self.column(n) for n in sizes],
            [self.column(total), self.whole(2 * blocks, self.rows // 2), self.column(blocks)]
            + self.pieces(),
            [struct((total, channels)), struct((2 * blocks, self.rows // 2)), struct((blocks, channels))]
            + [struct((p.shape[0], channels), BF16) for p in self.projected],
            [],
            100,
            self.projected + scanned[:4] + [enter, self.gain],
        )
        return outs[0], outs[1], outs[2], list(outs[3:])

    def scan_back(self, grads, state, stats):
        specs, shapes = self.scanned()
        return self.call(
            scan_back_kernel,
            "mixer_scan_back",
            self.pieces()
            + self.pieces(1)
            + self.pieces(2)
            + [
                pl.BlockSpec((p.shape[0], LANES), lambda i, last=p.shape[1] // LANES - 1: (0, last))
                for p in stats
            ]
            + [self.column(self.total)]
            + [self.column(1)] * 2,
            specs,
            shapes,
            [pltpu.VMEM((self.total, LANES), F32)],
            250,
            grads + self.projected * 2 + stats + [state, self.bound, self.gain],
        )

    def project_back(self, grads, state, stats, carry, scanned, enter):
        total, blocks, channels = self.total, self.blocks, self.channels
        sizes = [1, 1, blocks, total, total, blocks, blocks, blocks // 2]
        outs = self.call(
            project_back_kernel,
            "mixer_project_back",
            self.pieces()
            + self.pieces(0)
            + self.pieces(1)
            + self.pieces(2)
            + [
                pl.BlockSpec((p.shape[0], LANES), lambda i, last=p.shape[1] // LANES - 1: (0, last))
                for p in stats
            ]
            + [self.column(total)]
            + [self.column(n) for n in sizes],
            [self.whole(*p.shape) for p in self.projected] + [self.column(1)] * 2,
            [struct(p.shape, BF16) for p in self.projected] + [struct((1, channels))] * 2,
            [pltpu.VMEM((blocks, LANES), F32)],
            200,
            grads
            + self.projected * 3
            + stats
            + [state, self.bound, self.gain, carry]
            + scanned[:4]
            + [enter],
        )
        return list(outs[:-2]), outs[-2], outs[-1]


def strip_rows(first, last, start, size):
    split = first.shape[0]
    found = []
    if start < split:
        count = min(start + size, split) - start
        found.append((0, first[pl.ds(start, count), :]))
    if start + size > split:
        begin = max(start, split)
        found.append((begin - start, last[pl.ds(begin - split, start + size - begin), :]))
    return found


def place_glu_kernel(count, column_ref, *refs):
    out_ref, glu_ref = refs[-2:]
    size = out_ref.shape[1] // count
    for s in range(count):
        at = (column_ref[0] ^ s) * size
        for which in range(3):
            for offset, rows in strip_rows(refs[2 * s], refs[2 * s + 1], which * size, size):
                here = pl.ds(pl.multiple_of(at + offset, 16), rows.shape[0])
                if which == 0:
                    out_ref[0, here, :] = rows.astype(F32)
                else:
                    glu_ref[0, which - 1, here, :] = rows.astype(F32)


def place_mix_kernel(count, column_ref, *refs):
    out_ref, mix_ref, turn_ref = refs[-3:]
    size = out_ref.shape[1] // count
    for which in range(4):
        for s in range(count):
            at = (column_ref[0] ^ s) * size
            for offset, rows in strip_rows(refs[2 * s], refs[2 * s + 1], which * size, size):
                here = pl.ds(pl.multiple_of(at + offset, 16), rows.shape[0])
                if which == 3:
                    out_ref[0, here, :] = rows.astype(F32)
                else:
                    turn_ref[here, :] = rows.astype(F32)
        if which < 3:
            mix_ref[0, which] = turn_ref[...].T


def place_strips(body, name, layer, column, slots, kept, shapes, blocks, indices, scratch):
    flat = [v for halves in slots for v in halves]
    lanes = blocks[0][-1]
    kept = list(kept or ())
    return pl.pallas_call(
        functools.partial(body, len(slots)),
        name=name,
        grid=(flat[0].shape[1] // lanes,),
        in_specs=[pl.BlockSpec(memory_space=pltpu.SMEM)]
        + [pl.BlockSpec((v.shape[0], lanes), lambda i: (0, i)) for v in flat]
        + [pl.BlockSpec(memory_space=pl.ANY) for _ in kept],
        out_specs=[
            pl.BlockSpec(block, lambda i, index=index: (layer,) + index(i))
            for block, index in zip(blocks, indices)
        ],
        out_shape=[jax.ShapeDtypeStruct(shape, F32) for shape in shapes],
        scratch_shapes=scratch,
        input_output_aliases={1 + len(flat) + k: k for k in range(len(kept))},
        compiler_params=pltpu.CompilerParams(
            vmem_limit_bytes=VMEM_LIMIT, dimension_semantics=("arbitrary",)
        ),
        cost_estimate=pl.CostEstimate(flops=100, bytes_accessed=1024, transcendentals=0),
    )(column, *flat, *kept)


def matmul(a, b):
    return jnp.dot(a, b, preferred_element_type=F32)


def matmul_t(a, b):
    return lax.dot_general(a, b, (((1,), (1,)), ((), ())), preferred_element_type=F32)


def matmul_rows(a, b):
    return lax.dot_general(a, b, (((0,), (0,)), ((), ())), preferred_element_type=F32)


def rows_product(a, b):
    return matmul_rows(join(a), join(b)).astype(BF16)


@jax.tree_util.register_pytree_node_class
class Pair:
    def __init__(self, a, b):
        self.a, self.b = a, b

    @property
    def shape(self):
        return self.a.shape

    def __getitem__(self, part):
        return Pair(self.a[part], self.b[part])

    def tree_flatten(self):
        return (self.a, self.b), None

    @classmethod
    def tree_unflatten(cls, _, parts):
        return cls(*parts)


def rms_factor(values):
    return lax.rsqrt(jnp.mean(values * values, -1, keepdims=True) + norm_eps)


def rms_back(values, gain, grad):
    factor = rms_factor(values)
    normed = values * factor
    scaled = grad * gain
    back = factor * (scaled - normed * jnp.mean(scaled * normed, -1, keepdims=True))
    return back, jnp.sum(grad * normed, 0)


def bound_rows(logits):
    return jnp.cumsum(jax.nn.softmax(logits, 0), 0)


def local(
    hidden_in,
    cotangent,
    domain_tags,
    mix_weight,
    mix_out_weight,
    glu_weight,
    glu_out_weight,
    mix_gain,
    out_gain,
    glu_gain,
    bound_logits,
):
    dp = lax.axis_size("dp")
    line = lax.axis_size("mp") // 2
    column = lax.axis_index("dp")
    member = lax.axis_index("mp")
    core = member % 2
    core_arg = core.astype(jnp.int32).reshape(1)
    width = hidden_in.shape[1]
    layers = mix_weight.shape[0]
    channels = mix_weight.shape[3]
    units = glu_weight.shape[3]
    c_strip, u_strip = channels // dp, units // dp

    def cut(array, axis, size):
        return lax.dynamic_slice_in_dim(array, column * size, size, axis)

    scale_table = jnp.array(domain_scale, dtype=F32)
    match = domain_tags[0] == jnp.arange(3, dtype=jnp.int32)
    grad = cotangent.astype(F32) * jnp.sum(jnp.where(match, scale_table, 0.0))
    bound_vals, bound_back = jax.vjp(bound_rows, bound_logits)

    mix_w, out_w, gate_w, up_w, down_w = ([None] * layers for _ in range(5))

    def mix_strip(weight, out=None):
        strip = cut(weight, 2, c_strip).transpose(1, 2, 0).reshape(3 * c_strip, width)
        return strip if out is None else jnp.concatenate([strip, cut(out, 0, c_strip)], 0)

    def glu_strip(weight):
        return cut(weight, 2, u_strip).transpose(1, 2, 0).reshape(2 * u_strip, width)

    def gather_mix(l, strip, out=None):
        got = line_gather(strip)
        mixes = got[:, : 3 * c_strip].reshape(line, 3, c_strip, width).transpose(1, 0, 2, 3)
        mix_w[l] = mixes.reshape(3 * line * c_strip, width)
        out = got[:, 3 * c_strip :] if out is None else line_gather(out)
        out_w[l] = out.reshape(line * c_strip, width)

    def gather_glu(l, strip):
        got = line_gather(strip)
        gate_w[l] = got[:, :u_strip].reshape(line * u_strip, width)
        up_w[l] = got[:, u_strip:].reshape(line * u_strip, width)

    def gather_down(l, strip):
        down_w[l] = line_gather(strip).reshape(line * u_strip, width)

    strip = mix_strip(mix_weight[0])
    strip, hidden_in, out_strip = tie_all(strip, hidden_in, mix_out_weight[0])
    gather_mix(0, strip, cut(out_strip, 0, c_strip))
    half = hidden_in.shape[0] // 2

    def halves(rows):
        return [rows[:half], rows[half:]]

    def gathered(lows):
        return [piece for low in lows for piece in plane_gather(low)]

    def normed(rows, gain):
        return (rows * rms_factor(rows) * gain).astype(BF16)

    grad = halves(grad)
    stream = halves(hidden_in.astype(F32))
    kept = []
    for l in range(layers):
        stream_in = stream
        lows = [normed(rows, mix_gain[l]) for rows in stream]
        if l == 0:
            small = jnp.concatenate([cut(bound_vals, 1, c_strip), cut(out_gain, 1, c_strip)], 0)
            lows, small, first_glu = tie_all(lows, small, glu_weight[0])
            strip, down = tie_all(glu_strip(first_glu), glu_out_weight[0])
            gather_glu(0, strip)
            down_strip = cut(down, 0, u_strip)
            small = lax.dynamic_update_slice(
                jnp.zeros((small.shape[0], line, c_strip), F32), small[:, None], (0, member // 2, 0)
            )
            small = line_sum(small).reshape(-1, line * c_strip)
            bounds = [small[i : i + 1] for i in range(layers)]
            gains = [small[bound_vals.shape[0] + i :][:1] for i in range(layers)]
        mixer_in = gathered(lows)
        projected = [matmul_t(rows, mix_w[l]) for rows in mixer_in]
        mixer = Mixer(core_arg, projected, bounds[l], gains[l])
        scanned = mixer.scan()
        enter = line_carry(scanned[5], scanned[4], False)
        state, squares, carry, mixed = mixer.state(scanned, enter)
        if l + 1 < layers:
            down_strip, *raws = tie_all(
                down_strip, mix_weight[l + 1], mix_out_weight[l + 1], glu_weight[l + 1]
            )
            gather_down(l, down_strip)
            strip, raw = tie_all(mix_strip(*raws[:2]), raws[2])
            gather_mix(l + 1, strip)
            strip, down = tie_all(glu_strip(raw), glu_out_weight[l + 1])
            gather_glu(l + 1, strip)
            down_strip = cut(down, 0, u_strip)
        else:
            gather_down(l, down_strip)
        squares = plane_scatter_rows(
            squares.reshape(2, dp, 2, half).transpose(1, 2, 0, 3).reshape(dp, 2, 2 * half)
        )
        out_factor = halves(lax.rsqrt(squares / width + norm_eps)[:, None])
        raw = [
            plane_scatter(*mixed[2 * h : 2 * h + 2], lambda rows, w=out_w[l]: matmul(rows, w))[0]
            for h in (0, 1)
        ]
        stream_mid = [a + b * c for a, b, c in zip(stream, raw, out_factor)]
        glu_in = gathered([normed(rows, glu_gain[l]) for rows in stream_mid])

        def glu(rows):
            a, b = matmul_t(rows, gate_w[l]), matmul_t(rows, up_w[l])
            return a.astype(BF16), b.astype(BF16), (jax.nn.silu(a) * b).astype(BF16)

        if l == 0:
            glu_in, grad_low = tie_all(glu_in, [rows.astype(BF16) for rows in grad])
            last_grad = gathered(grad_low)
        gate, up, hidden = zip(*[glu(rows) for rows in glu_in])
        if l == 0:
            hidden, last_grad = tie_all(hidden, last_grad)
        stream = [
            stream_mid[h]
            + plane_scatter(*hidden[2 * h : 2 * h + 2], lambda rows, w=down_w[l]: matmul(rows, w))[0]
            for h in (0, 1)
        ]
        kept.append(
            (
                stream_in,
                mixer_in,
                mixer,
                state,
                carry,
                mixed,
                out_factor,
                raw,
                stream_mid,
                glu_in,
                gate,
                up,
                hidden,
            )
        )

    mix_gain_parts = [None] * layers
    glu_gain_parts = [None] * layers
    out_gain_parts = [None] * layers
    bound_parts = [None] * layers

    grads = {}

    def place(name, l, value):
        if name not in grads:
            grads[name] = jnp.zeros((layers,) + value.shape, F32)
        grads[name] = lax.dynamic_update_index_in_dim(grads[name], value.astype(F32), l, 0)

    column_arg = column.astype(jnp.int32).reshape(1)
    lanes = 512
    aligned = u_strip % 16 == 0 and width % lanes == 0

    def finish_glu(l, slots):
        if aligned:
            grads["glus"] = place_strips(
                place_glu_kernel,
                "place_glu",
                l,
                column_arg,
                slots,
                grads.get("glus"),
                [(layers, units, width), (layers, 2, units, width)],
                [(1, units, lanes), (1, 2, units, lanes)],
                [lambda i: (0, i), lambda i: (0, 0, i)],
                [],
            )
            grads["glu_out"] = grads["glus"][0]
            grads["glu"] = grads["glus"][1].transpose(0, 3, 1, 2)
            return
        strips = in_columns(slots)
        place("glu_out", l, strips[:, :u_strip].reshape(units, width))
        strips = strips[:, u_strip:].reshape(dp, 2, u_strip, width).transpose(3, 1, 0, 2)
        place("glu", l, strips.reshape(width, 2, units))

    def finish_mix(l, slots):
        grads["mixes"] = place_strips(
            place_mix_kernel,
            "place_mix",
            l,
            column_arg,
            slots,
            grads.get("mixes"),
            [(layers, channels, width), (layers, 3, width, channels)],
            [(1, channels, lanes), (1, 3, lanes, channels)],
            [lambda i: (0, i), lambda i: (0, i, 0)],
            [pltpu.VMEM((channels, lanes), F32)],
        )
        grads["mix_out"] = grads["mixes"][0]
        grads["mix"] = grads["mixes"][1].transpose(0, 2, 1, 3)

    for l in reversed(range(layers)):
        (
            stream_in,
            mixer_in,
            mixer,
            state,
            carry,
            mixed,
            out_factor,
            raw,
            stream_mid,
            glu_in,
            gate,
            up,
            hidden,
        ) = kept[l]
        if l == layers - 1:
            down_grad = last_grad
        else:
            down_grad = gathered([rows.astype(BF16) for rows in grad])
            down_grad, glu_sum = tie_all(down_grad, glu_sum)
            glu_strips = strips_near(glu_sum)

        def glu_back(rows, a, b):
            dhidden = matmul_t(rows, down_w[l])
            a, b = a.astype(F32), b.astype(F32)
            sig = jax.nn.sigmoid(a)
            dgate = (dhidden * b * sig * (1.0 + a * (1.0 - sig))).astype(BF16)
            return Pair(dgate, (dhidden * a * sig).astype(BF16))

        def glu_product(rows):
            return matmul(rows.a, gate_w[l]) + matmul(rows.b, up_w[l])

        pairs = [glu_back(*args) for args in zip(down_grad, gate, up)]
        back_first, _, _ = plane_scatter(*pairs[:2], glu_product)
        fill = (
            rows_product([p.a for p in pairs], glu_in),
            rows_product([p.b for p in pairs], glu_in),
        )
        if l < layers - 1:
            fill += (glu_strips,)
        back_last, down_part, fill = plane_scatter(
            *pairs[2:], glu_product, rows_product(hidden, down_grad), fill
        )
        gate_part, up_part = fill[:2]
        if l < layers - 1:
            glu_strips = fill[2]
        sent = [v.reshape(line, u_strip, width) for v in (down_part, gate_part, up_part)]
        sent = jnp.concatenate(sent, 1)
        back, gain_part = zip(
            *[rms_back(v, glu_gain[l], d) for v, d in zip(stream_mid, (back_first, back_last))]
        )
        glu_gain_parts[l] = sum(gain_part)
        grad = [a + b for a, b in zip(grad, back)]
        if l < layers - 1:
            sent, summed = tie_all(sent, summed)
        glu_sum = strip_halves(line_scatter(sent))

        lows = []
        for rows, factor, y in zip(grad, out_factor, raw):
            low = (rows * factor).astype(BF16)
            stat = jnp.mean(low.astype(F32) * y, -1) * (factor * factor)[:, 0]
            lows.append(jnp.concatenate([low, in_parts(stat)], 1))
        out_grad = gathered(lows)
        if l < layers - 1:
            glu_strips = strips_far(glu_strips)
            mix_strips = strips_far(strips_near(summed))
        padded = jnp.pad(out_w[l], ((0, 0), (0, LANES)))
        mixed_grad = [matmul_t(rows, padded) for rows in out_grad]
        scanned = mixer.scan_back(mixed_grad, state, out_grad)
        enter = line_carry(scanned[5], scanned[4], True)
        proj_grad, bound_parts[l], out_gain_parts[l] = mixer.project_back(
            mixed_grad, state, out_grad, carry, scanned, enter
        )
        out_part = rows_product(mixed, out_grad)[:, :width]
        mix_part = rows_product(proj_grad, mixer_in)

        def mix_sent(out_part, mix_part):
            mix_part = mix_part.reshape(3, line, c_strip, width).transpose(1, 0, 2, 3)
            mix_part = mix_part.reshape(line, 3 * c_strip, width)
            return jnp.concatenate([mix_part, out_part.reshape(line, c_strip, width)], 1)

        def mix_product(rows):
            return matmul(rows, mix_w[l])

        if l == 0:
            sent = mix_sent(out_part, mix_part)
            proj_grad, sent, glu_sum = tie_all(proj_grad, sent, glu_sum)
            proj_grad, glu_strips, mix_strips = tie_all(proj_grad, glu_strips, mix_strips)
            back_first, _, _ = plane_scatter(*proj_grad[:2], mix_product)
            finish_glu(1, glu_strips)
            finish_mix(1, mix_strips)
            fill = {name: grads[name] for name in ("glus", "mixes") if name in grads}
            back_last, _, fill = plane_scatter(*proj_grad[2:], mix_product, (), fill)
            grads.update(fill)
        else:
            back_first, _, _ = plane_scatter(*proj_grad[:2], mix_product)
            back_last, out_part, mix_part = plane_scatter(
                *proj_grad[2:], mix_product, out_part, mix_part
            )
            sent = mix_sent(out_part, mix_part)
        back, gain_part = zip(
            *[rms_back(v, mix_gain[l], d) for v, d in zip(stream_in, (back_first, back_last))]
        )
        mix_gain_parts[l] = sum(gain_part)
        grad = [a + b for a, b in zip(grad, back)]
        if l > 0:
            sent, glu_sum = tie_all(sent, glu_sum)
        summed = strip_halves(line_scatter(sent))
        if l == 0:
            grad, summed = tie_all(grad, summed)
    finish_glu(0, strips_far(strips_near(glu_sum)))
    mix_strips = strips_near(summed)

    def spread(row):
        zeros = jnp.zeros((line, 2, dp, c_strip), F32)
        return lax.dynamic_update_slice(
            zeros, row.reshape(line, 1, 1, c_strip), (0, core, column, 0)
        ).reshape(-1)

    rows = jnp.stack(
        mix_gain_parts
        + glu_gain_parts
        + [spread(v) for v in out_gain_parts]
        + [spread(v) for v in bound_parts]
    )
    rows, mix_strips = tie_all(rows, mix_strips)
    finish_mix(0, strips_far(mix_strips))
    rows = sum_all(rows)
    mix_gain_grad = rows[:layers]
    glu_gain_grad = rows[layers : 2 * layers]
    mine = lax.dynamic_slice_in_dim(rows[2 * layers :], member * channels, channels, 1)
    out_gain_grad = mine[:layers]
    extra = jnp.zeros((bound_vals.shape[0] - layers, channels), F32)
    bound_grad = bound_back(jnp.concatenate([mine[layers:], extra], 0))[0]
    return (
        jnp.concatenate(stream, 0),
        jnp.concatenate(grad, 0),
        grads["mix"],
        grads["mix_out"],
        grads["glu"],
        grads["glu_out"],
        mix_gain_grad,
        out_gain_grad,
        glu_gain_grad,
        bound_grad,
    )


def solution(mesh):
    return jax.shard_map(
        local,
        mesh=mesh,
        in_specs=(
            P(("dp", "mp"), None),
            P(("dp", "mp"), None),
            P("dp"),
            P(None, None, None, "mp"),
            P(None, "mp", None),
            P(None, None, None, "mp"),
            P(None, "mp", None),
            P(),
            P(None, "mp"),
            P(),
            P(None, "mp"),
        ),
        out_specs=(
            P(("dp", "mp"), None),
            P(("dp", "mp"), None),
            P(None, None, None, "mp"),
            P(None, "mp", None),
            P(None, None, None, "mp"),
            P(None, "mp", None),
            P(),
            P(None, "mp"),
            P(),
            P(None, "mp"),
        ),
        check_vma=False,
    )
```
